32 devices in a mesh: seq: 16 (over z, y, core), head: 2 (over x).
Axes of the slice: x: 2, y: 2, z: 4, core: 2. Of those that a mesh axis runs over, the one named last changes fastest.
Arguments:
- queries: bfloat16 [1024, 2048], P('seq', 'head'), may hold values from -15 to 15
- cache_keys: bfloat16 [2, 16384, 128], P('head', 'seq'), may hold values from -6 to 6
- cache_values: bfloat16 [2, 16384, 128], P('head', 'seq'), may hold values from -6 to 6
- new_keys: bfloat16 [1024, 256], P('seq', 'head'), may hold values from -9.5625 to 9.5625
- new_values: bfloat16 [1024, 256], P('seq', 'head'), may hold values from -6 to 6
- cache_len: int32 [16], P('seq'), may hold values from 256 to 1024, as said below
- span_rank: int32 [1024], replicated, may hold values from 0 to 1023, each once
- out_weight: bfloat16 [2048, 8192], P('head', 'seq'), may hold values from -0.125 to 0.125
Outputs:
- projected: bfloat16 [1024, 8192], P('head', 'seq')
The draws below stay inside these ranges and needn't reach their ends.
Inputs may be any that keep to these rules, and one draw needn't show every extreme that they name: `cache_len`: each shard holds at least 256 filled positions; one shard is full in every draw.
All inputs are finite; a program needn't handle non-finite values.
Results may differ from the reference program's by a relative error of at most 0.006.
Values may be sent and summed in bfloat16 or wider, within the bound.
A program may use at most 64 MiB of HBM per device.

```python
import math
import jax
import jax.numpy as jnp
from jax import lax

D = 8192
HD = 128
QPH = 8
KV_HEADS = 2
Q_HEADS = 16
SPAN_DEV = 64
SPAN = 1024
CACHE_DEV = 1024
SHARDS = 16
CONTEXT = 16384
BLOCK = 512


def draw_queries(key, part):
    key = jax.random.fold_in(key, 1)
    base = jnp.clip(2.5 * jax.random.normal(key, (SPAN, Q_HEADS, HD), jnp.float32), -15.0, 15.0)
    return base.reshape(SPAN, Q_HEADS * HD).astype(jnp.bfloat16)


def draw_cache_keys(key, part):
    key = jax.random.fold_in(key, 2)
    base = jnp.clip(jax.random.normal(key, (KV_HEADS, CONTEXT, HD), jnp.float32), -6.0, 6.0)
    return base.astype(jnp.bfloat16)


def draw_cache_len(key, part):
    key = jax.random.fold_in(key, 3)
    lengths = jax.random.randint(key, (SHARDS,), CACHE_DEV // 4, CACHE_DEV + 1)
    full_shard = jax.random.randint(jax.random.fold_in(key, 7), (), 0, SHARDS)
    return jnp.where(jnp.arange(SHARDS) == full_shard, CACHE_DEV, lengths).astype(jnp.int32)


def levels(key, shape, cuts, smallest, high):
    def one(dim, shards_of):
        steps = jax.random.uniform(jax.random.fold_in(jax.random.fold_in(key, 6), dim), (shards_of,), jnp.float32, smallest / len(cuts), high / len(cuts))
        return jnp.repeat(jnp.exp(steps), shape[dim] // shards_of).reshape((-1,) + (1,) * (len(shape) - dim - 1))

    level = one(*cuts[0])
    for cut in cuts[1:]:
        level = level * one(*cut)
    return level


def gaussian(own_key, extent, deviation, most, shards=(), held_as=jnp.bfloat16):
    loudness = levels(own_key, extent, shards, -0.22, 0.18) if shards else 1.0
    array = jax.random.normal(own_key, extent, jnp.float32) * deviation * loudness
    return jnp.minimum(jnp.maximum(array, -most), most).astype(held_as)


def setup_inputs(seed: int = 0) -> dict:
    arg_keys = jax.random.split(jax.random.key(seed), 9)
    queries = draw_queries(jax.random.fold_in(arg_keys[8], 71), 0)
    cache_keys = draw_cache_keys(jax.random.fold_in(arg_keys[8], 71), 0)
    cache_values = gaussian(arg_keys[2], (KV_HEADS, CONTEXT, HD), 1.0, 6.0, ((0, 2), (1, 16)))
    new_keys = gaussian(arg_keys[3], (SPAN, KV_HEADS * HD), 1.6, 9.5625, ((0, 16), (1, 2)))
    new_values = gaussian(arg_keys[4], (SPAN, KV_HEADS * HD), 1.0, 6.0, ((0, 16), (1, 2)))
    cache_len = draw_cache_len(jax.random.fold_in(arg_keys[8], 71), 0)
    span_rank = jax.random.permutation(arg_keys[6], SPAN).astype(jnp.int32)
    out_weight = gaussian(arg_keys[7], (Q_HEADS * HD, D), (Q_HEADS * HD) ** -0.5, 0.125, ((0, 2), (1, 16)))
    return dict(queries=queries, cache_keys=cache_keys, cache_values=cache_values, new_keys=new_keys, new_values=new_values, cache_len=cache_len, span_rank=span_rank, out_weight=out_weight)


NEG_FILL = -1e+30

def combine(earlier, latter):
    sum_a, max_a, tot_a = earlier
    sum_b, max_b, tot_b = latter
    overall = jnp.maximum(max_a, max_b)
    factor_a = jnp.exp(max_a - overall)
    factor_b = jnp.exp(max_b - overall)
    return (sum_a * factor_a[..., None] + sum_b * factor_b[..., None], overall, tot_a * factor_a + tot_b * factor_b)

def block_terms(query_rows, key_rows, value_rows, usable, score_scale):
    scores = jnp.dot(query_rows, key_rows.T, preferred_element_type=jnp.float32) * score_scale
    scores = jnp.where(usable, scores, NEG_FILL)
    row_max = lax.optimization_barrier(jnp.max(scores, axis=1))
    weights = jnp.where(usable, jnp.exp(scores - row_max[:, None]), 0.0).astype(jnp.bfloat16)
    row_sum = lax.optimization_barrier(jnp.sum(weights.astype(jnp.float32), axis=1))
    summed = jnp.dot(weights, value_rows, preferred_element_type=jnp.float32)
    return (summed, row_max, row_sum)

def reference(queries, cache_keys, cache_values, new_keys, new_values, cache_len, span_rank, out_weight):
    score_scale = jnp.float32(1.0 / math.sqrt(HD))
    row_total = SPAN * QPH
    blocks = CACHE_DEV // BLOCK
    rank_rows = jnp.repeat(span_rank, QPH)
    shard_rank = span_rank.reshape(SHARDS, SPAN_DEV)
    positions = jnp.arange(CACHE_DEV, dtype=jnp.int32)
    pieces = []
    for kv_head in range(KV_HEADS):
        query_rows = queries[:, kv_head * QPH * HD:(kv_head + 1) * QPH * HD].reshape(row_total, HD)
        shard_keys = cache_keys[kv_head].reshape(SHARDS, CACHE_DEV, HD)
        shard_values = cache_values[kv_head].reshape(SHARDS, CACHE_DEV, HD)
        span_keys = new_keys[:, kv_head * HD:(kv_head + 1) * HD].reshape(SHARDS, SPAN_DEV, HD)
        span_values = new_values[:, kv_head * HD:(kv_head + 1) * HD].reshape(SHARDS, SPAN_DEV, HD)

        def visit(running, inputs):
            key_rows, value_rows, length, new_key_rows, new_value_rows, new_rank = inputs
            scores = jnp.dot(query_rows, key_rows.T, preferred_element_type=jnp.float32) * score_scale
            usable = jnp.broadcast_to((positions < length).reshape(1, blocks, BLOCK), (row_total, blocks, BLOCK))
            scores = jnp.where(usable, scores.reshape(row_total, blocks, BLOCK), NEG_FILL)
            row_max = lax.optimization_barrier(jnp.max(scores, axis=2))
            weights = jnp.where(usable, jnp.exp(scores - row_max[..., None]), 0.0).astype(jnp.bfloat16)
            row_sum = lax.optimization_barrier(jnp.sum(weights.astype(jnp.float32), axis=2))
            summed = jnp.einsum('rnb,nbd->rnd', weights.astype(jnp.float32), value_rows.reshape(blocks, BLOCK, HD).astype(jnp.float32))
            for block_at in range(blocks):
                running = combine(running, (summed[:, block_at], row_max[:, block_at], row_sum[:, block_at]))
            usable_new = new_rank[None, :] <= rank_rows[:, None]
            running = combine(running, block_terms(query_rows, new_key_rows, new_value_rows, usable_new, score_scale))
            return (running, None)
        initial = (jnp.zeros((row_total, HD), jnp.float32), jnp.full((row_total,), NEG_FILL, jnp.float32), jnp.zeros((row_total,), jnp.float32))
        running, ignored = lax.scan(visit, initial, (shard_keys, shard_values, cache_len, span_keys, span_values, shard_rank))
        attended = (running[0] / running[2][:, None]).astype(jnp.bfloat16).reshape(SPAN, QPH * HD)
        pieces.append(attended)
    attended_all = jnp.concatenate(pieces, axis=1)
    return jnp.dot(attended_all, out_weight, preferred_element_type=jnp.float32).astype(jnp.bfloat16)
```

```python
import functools
import math

import jax
import jax.numpy as jnp
from jax import lax
from jax.experimental import pallas as pl
from jax.experimental.pallas import tpu as pltpu
from jax.sharding import PartitionSpec as P

MESH = pl.DeviceIdType.MESH
HD = 128
AUG = 144
PART = 136
FILL = -1e30
SCALE = math.log2(math.e) / math.sqrt(HD)
F32 = jnp.float32
BF16 = jnp.bfloat16


def dot(a, b):
    return jnp.dot(a, b, preferred_element_type=F32)


def kernel(
    zs_count, heads, toks, qph,
    q_ref, k_ref, v_ref, nk_ref, nv_ref, len_ref, rank_ref, w_ref, out_ref,
    qall, k1, v1, nkv, k2, v2, nkv_y, krank, part, corebuf, zsend, zrecv, aall, facc, xs, xr,
    qz_s, qz_r, qc_s, qc_r, kv_s, kv_r, pc_s, pc_r, pz_s, pz_r,
    az_s, az_r, ay_s, ay_r, ac_s, ac_r, ad_s, ad_r, x_s, x_r,
):
    cache = k_ref.shape[0]
    rows = toks * qph
    fresh = 2 * toks
    me = lax.axis_index("seq")
    my_head = lax.axis_index("head")
    c = lax.rem(me, 2)
    y = lax.rem(me // 2, 2)
    z = me // 4
    core_peer = me + 1 - 2 * c
    y_peer = me + 2 - 4 * y

    def seq_id(other):
        return {"seq": other}

    def zdev(other):
        return other * 4 + y * 2 + c

    barrier = pltpu.get_barrier_semaphore()
    pl.semaphore_signal(barrier, inc=1, device_id=seq_id(core_peer), device_id_type=MESH)
    pl.semaphore_signal(barrier, inc=1, device_id=seq_id(y_peer), device_id_type=MESH)
    for d in range(1, zs_count):
        pl.semaphore_signal(
            barrier, inc=1, device_id=seq_id(zdev(lax.rem(z + d, zs_count))), device_id_type=MESH
        )
    for e in range(1, heads):
        pl.semaphore_signal(
            barrier, inc=1, device_id={"head": lax.rem(my_head + e, heads)}, device_id_type=MESH
        )

    q_rows = jnp.concatenate([q_ref[:, h * HD:(h + 1) * HD] for h in range(qph)], axis=0)
    qall[z * 2 + c] = q_rows.astype(F32).T.astype(BF16)
    pl.semaphore_wait(barrier, zs_count + heads)

    def remote(src, dst, send, recv, device):
        return pltpu.make_async_remote_copy(
            src_ref=src, dst_ref=dst, send_sem=send, recv_sem=recv,
            device_id=device, device_id_type=MESH,
        )

    def q_to_z(d):
        slot = z * 2 + c
        return remote(
            qall.at[slot], qall.at[slot], qz_s.at[d], qz_r.at[d],
            seq_id(zdev(lax.rem(z + d, zs_count))),
        )

    def q_to_core(d):
        slot = lax.rem(z - d + zs_count, zs_count) * 2 + c
        return remote(qall.at[slot], qall.at[slot], qc_s.at[d], qc_r.at[d], seq_id(core_peer))

    q_to_core(0).start()
    for d in range(1, zs_count):
        q_to_z(d).start()

    length = len_ref[0]
    used = lax.broadcasted_iota(jnp.int32, (cache, HD), 0) < length
    k1[...] = jnp.where(used, k_ref[...].astype(F32), k_ref[0:1, :].astype(F32)).astype(BF16)
    nkv[0:toks] = nk_ref[...]
    nkv[toks:fresh] = nv_ref[...]
    k_to_y = remote(k1, k2.at[pl.ds(0, cache)], kv_s.at[0], kv_r.at[0], seq_id(y_peer))
    n_to_y = remote(nkv, nkv_y, kv_s.at[1], kv_r.at[1], seq_id(y_peer))
    v_to_y = remote(v1, v2.at[:, pl.ds(0, cache)], kv_s.at[2], kv_r.at[2], seq_id(y_peer))
    n_to_y.start()
    k_to_y.start()
    v1[0:HD] = jnp.where(used, v_ref[...].astype(F32), 0.0).T.astype(BF16)
    used_lane = lax.broadcasted_iota(jnp.int32, (AUG - HD, cache), 1) < length
    v1[HD:AUG] = jnp.where(used_lane, 1.0, 0.0).astype(BF16)
    v_to_y.start()

    lane = lax.broadcasted_iota(jnp.int32, (1, HD), 1)

    def chip_ranks(chip, half):
        row = rank_ref[pl.ds(chip, 1), :]
        turned = pltpu.roll(row, toks, 1)
        first = jnp.where(lane < toks, row, turned)
        second = jnp.where(lane < toks, turned, row)
        return jnp.where(half == 0, first, second).astype(F32)

    own_chip = z * 2 + y
    both = jnp.where(lane < toks, chip_ranks(own_chip, c), chip_ranks(z * 2 + 1 - y, c))
    krank[...] = jnp.broadcast_to(both, (HD, HD)).T

    half_rows = rows // 2

    def first_pass(slot):
        for half in range(2):
            cols = slice(half * half_rows, (half + 1) * half_rows)
            s = dot(k1[...], qall[slot, :, cols])
            top = jnp.max(s, axis=0, keepdims=True)
            weights = jnp.exp2((s - top) * SCALE).astype(BF16)
            summed = dot(v1[...], weights)
            part[slot, 0:HD, cols] = summed[0:HD]
            stat = lax.broadcasted_iota(jnp.int32, (8, half_rows), 0)
            part[slot, HD:PART, cols] = jnp.where(stat == 0, summed[HD:HD + 1], top)

    def second_pass(slot, zz, half_of):
        q_rank = chip_ranks(zz * 2 + y, half_of)
        q_rank = jnp.concatenate([q_rank] * (half_rows // HD), axis=1)
        k_rank = jnp.concatenate([krank[...]] * (half_rows // HD), axis=1)
        usable = k_rank <= q_rank
        for half in range(2):
            cols = slice(half * half_rows, (half + 1) * half_rows)
            qt = qall[slot, :, cols]
            s = dot(k2[0:cache], qt)
            s_new = jnp.where(usable, dot(k2[cache:cache + fresh], qt), FILL)
            top_1 = part[slot, HD + 1:HD + 2, cols]
            sum_1 = part[slot, HD:HD + 1, cols]
            top = jnp.maximum(jnp.max(s, axis=0, keepdims=True), top_1)
            top = jnp.maximum(top, jnp.max(s_new, axis=0, keepdims=True))
            weights = jnp.exp2((s - top) * SCALE).astype(BF16)
            weights_new = jnp.exp2((s_new - top) * SCALE).astype(BF16)
            summed = dot(v2[:, 0:cache], weights) + dot(v2[:, cache:cache + fresh], weights_new)
            keep = jnp.exp2((top_1 - top) * SCALE)
            part[slot, 0:HD, cols] = part[slot, 0:HD, cols] * keep + summed[0:HD]
            total = sum_1 * keep + summed[HD:HD + 1]
            stat = lax.broadcasted_iota(jnp.int32, (8, half_rows), 0)
            part[slot, HD:PART, cols] = jnp.where(stat == 0, total, top)

    def pass_one(d, carry):
        zz = lax.rem(z - d + zs_count, zs_count)

        @pl.when(d > 0)
        def _():
            q_to_z(d).wait_recv()
            q_to_core(d).start()

        first_pass(zz * 2 + c)
        q_to_core(d).wait_recv()
        first_pass(zz * 2 + 1 - c)
        return carry

    lax.fori_loop(0, zs_count, pass_one, 0)

    n_to_y.wait_recv()
    k_to_y.wait_recv()
    k2[cache:cache + toks] = nkv[0:toks]
    k2[cache + toks:cache + fresh] = nkv_y[0:toks]
    new_values = jnp.concatenate([nkv[toks:fresh], nkv_y[toks:fresh]], axis=0)
    v_to_y.wait_recv()
    v2[0:HD, cache:cache + fresh] = new_values.astype(F32).T.astype(BF16)
    v2[HD:AUG, cache:cache + fresh] = jnp.ones((AUG - HD, fresh), BF16)

    def p_to_core(d):
        zz = lax.rem(z - d + zs_count, zs_count)
        at = d - 1
        return remote(
            part.at[zz * 2 + 1 - c], corebuf.at[at], pc_s.at[at], pc_r.at[at], seq_id(core_peer)
        )

    def p_to_z(d):
        zz = lax.rem(z - d + zs_count, zs_count)
        return remote(zsend.at[d], zrecv.at[d], pz_s.at[d], pz_r.at[d], seq_id(zdev(zz)))

    def merged(slot, at):
        sum_a, top_a = part[slot, HD:HD + 1, :], part[slot, HD + 1:HD + 2, :]
        sum_b, top_b = corebuf[at, HD:HD + 1, :], corebuf[at, HD + 1:HD + 2, :]
        top = jnp.maximum(top_a, top_b)
        fac_a = jnp.exp2((top_a - top) * SCALE)
        fac_b = jnp.exp2((top_b - top) * SCALE)
        total = sum_a * fac_a + sum_b * fac_b
        level = top * SCALE + jnp.log2(total)
        inverse = 1.0 / total
        mean = part[slot, 0:HD, :] * (fac_a * inverse) + corebuf[at, 0:HD, :] * (fac_b * inverse)
        return mean, level

    def pass_two(d, carry):
        zz = lax.rem(z - d + zs_count, zs_count)
        second_pass(zz * 2 + 1 - c, zz, 1 - c)
        p_to_core(d).start()
        second_pass(zz * 2 + c, zz, c)
        p_to_core(d).wait_recv()

        @pl.when(d < zs_count)
        def _():
            mean, level = merged(zz * 2 + c, d - 1)
            zsend[d, 0:HD] = mean.astype(BF16)
            high = level.astype(BF16).astype(F32)
            middle = (level - high).astype(BF16).astype(F32)
            low = level - high - middle
            stat = lax.broadcasted_iota(jnp.int32, (AUG - HD, rows), 0)
            terms = jnp.where(stat == 0, high, jnp.where(stat == 1, middle, low))
            zsend[d, HD:AUG] = terms.astype(BF16)
            p_to_z(d).start()

        return carry

    lax.fori_loop(1, zs_count + 1, pass_two, 0)

    means, levels = [], []
    mean, level = merged(z * 2 + c, zs_count - 1)
    means.append(mean)
    levels.append(level)
    for d in range(1, zs_count):
        p_to_z(d).wait_recv()
        terms = zrecv[d, HD:AUG].astype(F32)
        levels.append(terms[0:1] + terms[1:2] + terms[2:3])
        means.append(zrecv[d, 0:HD].astype(F32))
    top = functools.reduce(jnp.maximum, levels)
    factors = [jnp.exp2(level - top) for level in levels]
    inverse = 1.0 / sum(factors)
    attended = sum(mean * (factor * inverse) for mean, factor in zip(means, factors))
    attended = attended.T.astype(BF16)
    own = pl.ds(pl.multiple_of(me * toks, toks), toks)
    for h in range(qph):
        aall[own, h * HD:(h + 1) * HD] = attended[h * toks:(h + 1) * toks]

    chip_rows = 4 * toks
    per_head = zs_count // heads

    def spot(zz, yy, cc):
        return pl.ds(pl.multiple_of((zz * 4 + yy * 2 + cc) * toks, toks), toks)

    def back(d):
        return lax.rem(z - d + zs_count, zs_count)

    def a_to_z(d):
        where = spot(z, y, c)
        return remote(
            aall.at[where], aall.at[where], az_s.at[d], az_r.at[d],
            seq_id(zdev(lax.rem(z + d, zs_count))),
        )

    def a_to_y(d):
        where = spot(back(d), y, c)
        return remote(aall.at[where], aall.at[where], ay_s.at[d], ay_r.at[d], seq_id(y_peer))

    def a_to_core(d):
        where = spot(back(d), y, c)
        return remote(aall.at[where], aall.at[where], ac_s.at[d], ac_r.at[d], seq_id(core_peer))

    def ay_to_core(d):
        where = spot(back(d), 1 - y, c)
        return remote(aall.at[where], aall.at[where], ad_s.at[d], ad_r.at[d], seq_id(core_peer))

    def x_send(d):
        zz = back(d)
        owner = zz // per_head
        slot = lax.rem(my_head - owner + heads, heads) * per_head + lax.rem(zz, per_head)
        return remote(xs.at[d], xr.at[slot], x_s.at[d], x_r.at[slot], {"head": owner})

    for d in range(1, zs_count):
        a_to_z(d).start()

    def spread(i, carry):
        @pl.when(i < zs_count)
        def _():
            @pl.when(i > 0)
            def _():
                a_to_z(i).wait_recv()

            a_to_y(i).start()
            a_to_core(i).start()

        @pl.when(jnp.logical_and(i >= 1, i <= zs_count))
        def _():
            a_to_y(i - 1).wait_recv()
            ay_to_core(i - 1).start()

        @pl.when(i >= 2)
        def _():
            d = i - 2
            a_to_core(d).wait_recv()
            ay_to_core(d).wait_recv()
            zz = back(d)
            lines = pl.ds(pl.multiple_of(zz * chip_rows, chip_rows), chip_rows)
            result = dot(aall[lines, :], w_ref[...])
            mine = zz // per_head == my_head

            @pl.when(mine)
            def _():
                facc[lax.rem(zz, per_head)] = result

            @pl.when(jnp.logical_not(mine))
            def _():
                xs[d] = result.astype(BF16)
                x_send(d).start()

        return carry

    lax.fori_loop(0, zs_count + 2, spread, 0)

    for k in range(per_head):
        total = facc[k]
        for e in range(1, heads):
            slot = e * per_head + k
            remote(
                xs.at[0], xr.at[slot], x_s.at[0], x_r.at[slot],
                {"head": lax.rem(my_head + e, heads)},
            ).wait_recv()
            total = total + xr[slot].astype(F32)
        out_ref[k * chip_rows:(k + 1) * chip_rows] = total.astype(BF16)

    n_to_y.wait_send()
    k_to_y.wait_send()
    v_to_y.wait_send()

    def finish(d, carry):
        q_to_core(d).wait_send()
        p_to_core(d + 1).wait_send()
        a_to_y(d).wait_send()
        a_to_core(d).wait_send()
        ay_to_core(d).wait_send()

        @pl.when(d > 0)
        def _():
            q_to_z(d).wait_send()
            p_to_z(d).wait_send()
            a_to_z(d).wait_send()

        @pl.when(back(d) // per_head != my_head)
        def _():
            x_send(d).wait_send()

        return carry

    lax.fori_loop(0, zs_count, finish, 0)


def body(queries, cache_keys, cache_values, new_keys, new_values, cache_len, span_rank, out_weight):
    toks = queries.shape[0]
    qph = queries.shape[1] // HD
    cache = cache_keys.shape[1]
    rows = toks * qph
    width = out_weight.shape[1]
    shards = lax.axis_size("seq")
    heads = lax.axis_size("head")
    zs = shards // 4
    span = span_rank.shape[0]
    out_rows = span // heads
    vmem = pl.BlockSpec(memory_space=pltpu.VMEM)
    smem = pl.BlockSpec(memory_space=pltpu.SMEM)
    sems = [zs, zs, zs, zs, 3, 3, zs, zs, zs, zs] + [zs] * 8 + [zs, zs]
    per_head = zs // heads
    return pl.pallas_call(
        functools.partial(kernel, zs, heads, toks, qph),
        out_shape=jax.ShapeDtypeStruct((out_rows, width), BF16),
        in_specs=[vmem] * 5 + [smem] + [vmem] * 2,
        out_specs=vmem,
        scratch_shapes=[
            pltpu.VMEM((zs * 2, HD, rows), BF16),
            pltpu.VMEM((cache, HD), BF16),
            pltpu.VMEM((AUG, cache), BF16),
            pltpu.VMEM((2 * toks, HD), BF16),
            pltpu.VMEM((cache + 2 * toks, HD), BF16),
            pltpu.VMEM((AUG, cache + 2 * toks), BF16),
            pltpu.VMEM((2 * toks, HD), BF16),
            pltpu.VMEM((HD, HD), F32),
            pltpu.VMEM((zs * 2, PART, rows), F32),
            pltpu.VMEM((zs, PART, rows), F32),
            pltpu.VMEM((zs, AUG, rows), BF16),
            pltpu.VMEM((zs, AUG, rows), BF16),
            pltpu.VMEM((span, qph * HD), BF16),
            pltpu.VMEM((per_head, 4 * toks, width), F32),
            pltpu.VMEM((zs, 4 * toks, width), BF16),
            pltpu.VMEM((zs, 4 * toks, width), BF16),
        ] + [pltpu.SemaphoreType.DMA((count,)) for count in sems],
        compiler_params=pltpu.CompilerParams(
            collective_id=0, has_side_effects=True, vmem_limit_bytes=56 * 1024 * 1024
        ),
    )(
        queries, cache_keys[0], cache_values[0], new_keys, new_values, cache_len,
        span_rank.reshape(span // HD, HD), out_weight,
    )


def solution(mesh):
    return jax.shard_map(
        body,
        mesh=mesh,
        in_specs=(
            P("seq", "head"),
            P("head", "seq", None),
            P("head", "seq", None),
            P("seq", "head"),
            P("seq", "head"),
            P("seq"),
            P(),
            P("head", "seq"),
        ),
        out_specs=P("head", "seq"),
        check_vma=False,
    )
```

```python
import functools
import math

import jax
import jax.numpy as jnp
from jax import lax
from jax.experimental import pallas as pl
from jax.experimental.pallas import tpu as pltpu
from jax.sharding import PartitionSpec as P

MESH = pl.DeviceIdType.MESH
HD = 128
AUG = 144
PART = 136
FILL = -1e30
SCALE = math.log2(math.e) / math.sqrt(HD)
F32 = jnp.float32
BF16 = jnp.bfloat16


def dot(a, b):
    return jnp.dot(a, b, preferred_element_type=F32)


def kernel(
    zs_count, heads, toks, qph,
    q_ref, k_ref, v_ref, nk_ref, nv_ref, len_ref, rank_ref, w_ref, out_ref,
    qall, k1, v1, nkv, k2, v2, nkv_y, krank, part, corebuf, zsend, zrecv, aall, facc, xs, xr,
    qz_s, qz_r, qc_s, qc_r, kv_s, kv_r, pc_s, pc_r, pz_s, pz_r,
    az_s, az_r, ay_s, ay_r, ac_s, ac_r, ad_s, ad_r, x_s, x_r,
):
    cache = k_ref.shape[0]
    rows = toks * qph
    fresh = 2 * toks
    me = lax.axis_index("seq")
    my_head = lax.axis_index("head")
    c = lax.rem(me, 2)
    y = lax.rem(me // 2, 2)
    z = me // 4
    core_peer = me + 1 - 2 * c
    y_peer = me + 2 - 4 * y

    def seq_id(other):
        return {"seq": other}

    def zdev(other):
        return other * 4 + y * 2 + c

    barrier = pltpu.get_barrier_semaphore()
    pl.semaphore_signal(barrier, inc=1, device_id=seq_id(core_peer), device_id_type=MESH)
    pl.semaphore_signal(barrier, inc=1, device_id=seq_id(y_peer), device_id_type=MESH)
    for d in range(1, zs_count):
        pl.semaphore_signal(
            barrier, inc=1, device_id=seq_id(zdev(lax.rem(z + d, zs_count))), device_id_type=MESH
        )
    for e in range(1, heads):
        pl.semaphore_signal(
            barrier, inc=1, device_id={"head": lax.rem(my_head + e, heads)}, device_id_type=MESH
        )

    q_rows = jnp.concatenate([q_ref[:, h * HD:(h + 1) * HD] for h in range(qph)], axis=0)
    qall[z * 2 + c] = q_rows.astype(F32).T.astype(BF16)
    pl.semaphore_wait(barrier, zs_count + heads)

    def remote(src, dst, send, recv, device):
        return pltpu.make_async_remote_copy(
            src_ref=src, dst_ref=dst, send_sem=send, recv_sem=recv,
            device_id=device, device_id_type=MESH,
        )

    def q_to_z(d):
        slot = z * 2 + c
        return remote(
            qall.at[slot], qall.at[slot], qz_s.at[d], qz_r.at[d],
            seq_id(zdev(lax.rem(z + d, zs_count))),
        )

    def q_to_core(d):
        slot = lax.rem(z - d + zs_count, zs_count) * 2 + c
        return remote(qall.at[slot], qall.at[slot], qc_s.at[d], qc_r.at[d], seq_id(core_peer))

    q_to_core(0).start()
    for d in range(1, zs_count):
        q_to_z(d).start()

    length = len_ref[0]
    used = lax.broadcasted_iota(jnp.int32, (cache, HD), 0) < length
    k1[...] = jnp.where(used, k_ref[...].astype(F32), k_ref[0:1, :].astype(F32)).astype(BF16)
    nkv[0:toks] = nk_ref[...]
    nkv[toks:fresh] = nv_ref[...]
    k_to_y = remote(k1, k2.at[pl.ds(0, cache)], kv_s.at[0], kv_r.at[0], seq_id(y_peer))
    n_to_y = remote(nkv, nkv_y, kv_s.at[1], kv_r.at[1], seq_id(y_peer))
    v_to_y = remote(v1, v2.at[:, pl.ds(0, cache)], kv_s.at[2], kv_r.at[2], seq_id(y_peer))
    n_to_y.start()
    k_to_y.start()
    v1[0:HD] = jnp.where(used, v_ref[...].astype(F32), 0.0).T.astype(BF16)
    used_lane = lax.broadcasted_iota(jnp.int32, (AUG - HD, cache), 1) < length
    v1[HD:AUG] = jnp.where(used_lane, 1.0, 0.0).astype(BF16)
    v_to_y.start()

    lane = lax.broadcasted_iota(jnp.int32, (1, HD), 1)

    def chip_ranks(chip, half):
        row = rank_ref[pl.ds(chip, 1), :]
        turned = pltpu.roll(row, toks, 1)
        first = jnp.where(lane < toks, row, turned)
        second = jnp.where(lane < toks, turned, row)
        return jnp.where(half == 0, first, second).astype(F32)

    own_chip = z * 2 + y
    both = jnp.where(lane < toks, chip_ranks(own_chip, c), chip_ranks(z * 2 + 1 - y, c))
    krank[...] = jnp.broadcast_to(both, (HD, HD)).T

    half_rows = rows // 2

    def first_pass(slot):
        for half in range(2):
            cols = slice(half * half_rows, (half + 1) * half_rows)
            s = dot(k1[...], qall[slot, :, cols])
            top = jnp.max(s, axis=0, keepdims=True)
            weights = jnp.exp2((s - top) * SCALE).astype(BF16)
            summed = dot(v1[...], weights)
            part[slot, 0:HD, cols] = summed[0:HD]
            stat = lax.broadcasted_iota(jnp.int32, (8, half_rows), 0)
            part[slot, HD:PART, cols] = jnp.where(stat == 0, summed[HD:HD + 1], top)

    def second_pass(slot, zz, half_of):
        q_rank = chip_ranks(zz * 2 + y, half_of)
        q_rank = jnp.concatenate([q_rank] * (half_rows // HD), axis=1)
        k_rank = jnp.concatenate([krank[...]] * (half_rows // HD), axis=1)
        usable = k_rank <= q_rank
        for half in range(2):
            cols = slice(half * half_rows, (half + 1) * half_rows)
            qt = qall[slot, :, cols]
            s = dot(k2[0:cache], qt)
            s_new = jnp.where(usable, dot(k2[cache:cache + fresh], qt), FILL)
            top_1 = part[slot, HD + 1:HD + 2, cols]
            sum_1 = part[slot, HD:HD + 1, cols]
            top = jnp.maximum(jnp.max(s, axis=0, keepdims=True), top_1)
            top = jnp.maximum(top, jnp.max(s_new, axis=0, keepdims=True))
            weights = jnp.exp2((s - top) * SCALE).astype(BF16)
            weights_new = jnp.exp2((s_new - top) * SCALE).astype(BF16)
            summed = dot(v2[:, 0:cache], weights) + dot(v2[:, cache:cache + fresh], weights_new)
            keep = jnp.exp2((top_1 - top) * SCALE)
            part[slot, 0:HD, cols] = part[slot, 0:HD, cols] * keep + summed[0:HD]
            total = sum_1 * keep + summed[HD:HD + 1]
            stat = lax.broadcasted_iota(jnp.int32, (8, half_rows), 0)
            part[slot, HD:PART, cols] = jnp.where(stat == 0, total, top)

    def pass_one(d, carry):
        zz = lax.rem(z - d + zs_count, zs_count)

        @pl.when(d > 0)
        def _():
            q_to_z(d).wait_recv()
            q_to_core(d).start()

        first_pass(zz * 2 + c)
        q_to_core(d).wait_recv()
        first_pass(zz * 2 + 1 - c)
        return carry

    lax.fori_loop(0, zs_count, pass_one, 0)

    n_to_y.wait_recv()
    k_to_y.wait_recv()
    k2[cache:cache + toks] = nkv[0:toks]
    k2[cache + toks:cache + fresh] = nkv_y[0:toks]
    new_values = jnp.concatenate([nkv[toks:fresh], nkv_y[toks:fresh]], axis=0)
    v_to_y.wait_recv()
    v2[0:HD, cache:cache + fresh] = new_values.astype(F32).T.astype(BF16)
    v2[HD:AUG, cache:cache + fresh] = jnp.ones((AUG - HD, fresh), BF16)

    def p_to_core(d):
        zz = lax.rem(z - d + zs_count, zs_count)
        at = d - 1
        return remote(
            part.at[zz * 2 + 1 - c], corebuf.at[at], pc_s.at[at], pc_r.at[at], seq_id(core_peer)
        )

    def p_to_z(d):
        zz = lax.rem(z - d + zs_count, zs_count)
        return remote(zsend.at[d], zrecv.at[d], pz_s.at[d], pz_r.at[d], seq_id(zdev(zz)))

    def merged(slot, at):
        sum_a, top_a = part[slot, HD:HD + 1, :], part[slot, HD + 1:HD + 2, :]
        sum_b, top_b = corebuf[at, HD:HD + 1, :], corebuf[at, HD + 1:HD + 2, :]
        top = jnp.maximum(top_a, top_b)
        fac_a = jnp.exp2((top_a - top) * SCALE)
        fac_b = jnp.exp2((top_b - top) * SCALE)
        total = sum_a * fac_a + sum_b * fac_b
        level = top * SCALE + jnp.log2(total)
        inverse = 1.0 / total
        mean = part[slot, 0:HD, :] * (fac_a * inverse) + corebuf[at, 0:HD, :] * (fac_b * inverse)
        return mean, level

    def pass_two(d, carry):
        zz = lax.rem(z - d + zs_count, zs_count)
        second_pass(zz * 2 + 1 - c, zz, 1 - c)
        p_to_core(d).start()
        second_pass(zz * 2 + c, zz, c)
        p_to_core(d).wait_recv()

        @pl.when(d < zs_count)
        def _():
            mean, level = merged(zz * 2 + c, d - 1)
            zsend[d, 0:HD] = mean.astype(BF16)
            high = level.astype(BF16).astype(F32)
            middle = (level - high).astype(BF16).astype(F32)
            low = level - high - middle
            stat = lax.broadcasted_iota(jnp.int32, (AUG - HD, rows), 0)
            terms = jnp.where(stat == 0, high, jnp.where(stat == 1, middle, low))
            zsend[d, HD:AUG] = terms.astype(BF16)
            p_to_z(d).start()

        return carry

    lax.fori_loop(1, zs_count + 1, pass_two, 0)

    means, levels = [], []
    mean, level = merged(z * 2 + c, zs_count - 1)
    means.append(mean)
    levels.append(level)
    for d in range(1, zs_count):
        p_to_z(d).wait_recv()
        terms = zrecv[d, HD:AUG].astype(F32)
        levels.append(terms[0:1] + terms[1:2] + terms[2:3])
        means.append(zrecv[d, 0:HD].astype(F32))
    top = functools.reduce(jnp.maximum, levels)
    factors = [jnp.exp2(level - top) for level in levels]
    inverse = 1.0 / sum(factors)
    attended = sum(mean * (factor * inverse) for mean, factor in zip(means, factors))
    attended = attended.T.astype(BF16)
    own = pl.ds(pl.multiple_of(me * toks, toks), toks)
    for h in range(qph):
        aall[own, h * HD:(h + 1) * HD] = attended[h * toks:(h + 1) * toks]

    chip_rows = 4 * toks
    per_head = zs_count // heads

    def spot(zz, yy, cc):
        return pl.ds(pl.multiple_of((zz * 4 + yy * 2 + cc) * toks, toks), toks)

    def a_move(s, step):
        where = spot(s, y, c)
        side = 0 if step > 0 else 1
        return remote(
            aall.at[where], aall.at[where], az_s.at[side, s], az_r.at[s], seq_id(zdev(z + step))
        )

    def a_to_y(s):
        where = spot(s, y, c)
        return remote(aall.at[where], aall.at[where], ay_s.at[s], ay_r.at[s], seq_id(y_peer))

    def a_to_core(s):
        where = spot(s, y, c)
        return remote(aall.at[where], aall.at[where], ac_s.at[s], ac_r.at[s], seq_id(core_peer))

    def ay_to_core(s):
        where = spot(s, 1 - y, c)
        return remote(aall.at[where], aall.at[where], ad_s.at[s], ad_r.at[s], seq_id(core_peer))

    def x_send(s):
        owner = s // per_head
        slot = lax.rem(my_head - owner + heads, heads) * per_head + lax.rem(s, per_head)
        return remote(xs.at[s], xr.at[slot], x_s.at[s], x_r.at[slot], {"head": owner})

    def product(s):
        lines = pl.ds(pl.multiple_of(s * chip_rows, chip_rows), chip_rows)
        return dot(aall[lines, :], w_ref[...])

    @pl.when(z < zs_count - 1)
    def _():
        a_move(z, 1).start()

    @pl.when(z > 0)
    def _():
        a_move(z, -1).start()

    a_to_y(z).start()
    a_to_core(z).start()

    def spread(i, carry):
        for step in (1, -1):
            s = z - step * i
            here = jnp.logical_and(s >= 0, s < zs_count)

            @pl.when(jnp.logical_and(here, i < zs_count))
            def _():
                a_move(s, step).wait_recv()
                onward = z < zs_count - 1 if step > 0 else z > 0

                @pl.when(onward)
                def _():
                    a_move(s, step).start()

                a_to_y(s).start()
                a_to_core(s).start()

        for step in (1, -1):
            s = z - step * (i - 1)
            here = jnp.logical_and(s >= 0, s < zs_count)
            if step < 0:
                here = jnp.logical_and(here, i > 1)

            @pl.when(here)
            def _():
                a_to_y(s).wait_recv()
                ay_to_core(s).start()

        for step in (1, -1):
            s = z - step * (i - 2)
            here = jnp.logical_and(jnp.logical_and(s >= 0, s < zs_count), i >= 2)
            if step < 0:
                here = jnp.logical_and(here, i > 2)

            @pl.when(jnp.logical_and(here, s // per_head != my_head))
            def _():
                a_to_core(s).wait_recv()
                ay_to_core(s).wait_recv()
                xs[s] = product(s).astype(BF16)
                x_send(s).start()

        return carry

    lax.fori_loop(1, zs_count + 2, spread, 0)

    for k in range(per_head):
        s = my_head * per_head + k
        a_to_core(s).wait_recv()
        ay_to_core(s).wait_recv()
        facc[k] = product(s)

    for k in range(per_head):
        total = facc[k]
        for e in range(1, heads):
            slot = e * per_head + k
            remote(
                xs.at[0], xr.at[slot], x_s.at[0], x_r.at[slot],
                {"head": lax.rem(my_head + e, heads)},
            ).wait_recv()
            total = total + xr[slot].astype(F32)
        out_ref[k * chip_rows:(k + 1) * chip_rows] = total.astype(BF16)

    n_to_y.wait_send()
    k_to_y.wait_send()
    v_to_y.wait_send()

    def finish(d, carry):
        q_to_core(d).wait_send()
        p_to_core(d + 1).wait_send()
        a_to_y(d).wait_send()
        a_to_core(d).wait_send()
        ay_to_core(d).wait_send()

        @pl.when(d > 0)
        def _():
            q_to_z(d).wait_send()
            p_to_z(d).wait_send()

        @pl.when(jnp.logical_and(z < zs_count - 1, d <= z))
        def _():
            a_move(d, 1).wait_send()

        @pl.when(jnp.logical_and(z > 0, d >= z))
        def _():
            a_move(d, -1).wait_send()

        @pl.when(d // per_head != my_head)
        def _():
            x_send(d).wait_send()

        return carry

    lax.fori_loop(0, zs_count, finish, 0)


def body(queries, cache_keys, cache_values, new_keys, new_values, cache_len, span_rank, out_weight):
    toks = queries.shape[0]
    qph = queries.shape[1] // HD
    cache = cache_keys.shape[1]
    rows = toks * qph
    width = out_weight.shape[1]
    shards = lax.axis_size("seq")
    heads = lax.axis_size("head")
    zs = shards // 4
    span = span_rank.shape[0]
    out_rows = span // heads
    vmem = pl.BlockSpec(memory_space=pltpu.VMEM)
    smem = pl.BlockSpec(memory_space=pltpu.SMEM)
    sems = [(zs,)] * 4 + [(3,)] * 2 + [(zs,)] * 4 + [(2, zs)] + [(zs,)] * 9
    per_head = zs // heads
    return pl.pallas_call(
        functools.partial(kernel, zs, heads, toks, qph),
        out_shape=jax.ShapeDtypeStruct((out_rows, width), BF16),
        in_specs=[vmem] * 5 + [smem] + [vmem] * 2,
        out_specs=vmem,
        scratch_shapes=[
            pltpu.VMEM((zs * 2, HD, rows), BF16),
            pltpu.VMEM((cache, HD), BF16),
            pltpu.VMEM((AUG, cache), BF16),
            pltpu.VMEM((2 * toks, HD), BF16),
            pltpu.VMEM((cache + 2 * toks, HD), BF16),
            pltpu.VMEM((AUG, cache + 2 * toks), BF16),
            pltpu.VMEM((2 * toks, HD), BF16),
            pltpu.VMEM((HD, HD), F32),
            pltpu.VMEM((zs * 2, PART, rows), F32),
            pltpu.VMEM((zs, PART, rows), F32),
            pltpu.VMEM((zs, AUG, rows), BF16),
            pltpu.VMEM((zs, AUG, rows), BF16),
            pltpu.VMEM((span, qph * HD), BF16),
            pltpu.VMEM((per_head, 4 * toks, width), F32),
            pltpu.VMEM((zs, 4 * toks, width), BF16),
            pltpu.VMEM((zs, 4 * toks, width), BF16),
        ] + [pltpu.SemaphoreType.DMA(count) for count in sems],
        compiler_params=pltpu.CompilerParams(
            collective_id=0, has_side_effects=True, vmem_limit_bytes=56 * 1024 * 1024
        ),
    )(
        queries, cache_keys[0], cache_values[0], new_keys, new_values, cache_len,
        span_rank.reshape(span // HD, HD), out_weight,
    )


def solution(mesh):
    return jax.shard_map(
        body,
        mesh=mesh,
        in_specs=(
            P("seq", "head"),
            P("head", "seq", None),
            P("head", "seq", None),
            P("seq", "head"),
            P("seq", "head"),
            P("seq"),
            P(),
            P("head", "seq"),
        ),
        out_specs=P("head", "seq"),
        check_vma=False,
    )
```

```python
import functools
import math

import jax
import jax.numpy as jnp
from jax import lax
from jax.experimental import pallas as pl
from jax.experimental.pallas import tpu as pltpu
from jax.sharding import PartitionSpec as P

MESH = pl.DeviceIdType.MESH
HD = 128
AUG = 144
PART = 136
FILL = -1e30
SCALE = math.log2(math.e) / math.sqrt(HD)
F32 = jnp.float32
BF16 = jnp.bfloat16


def dot(a, b):
    return jnp.dot(a, b, preferred_element_type=F32)


def kernel(
    zs_count, heads, toks, qph,
    q_ref, k_ref, v_ref, nk_ref, nv_ref, len_ref, rank_ref, w_ref, out_ref,
    qall, k1, v1, nkv, k2, v2, nkv_y, krank, part, corebuf, zsend, zrecv, aall, facc, xs, xr,
    s0, s1, s2, s3, p0, p1, p2, p3,
    qz_s, qz_r, qc_s, qc_r, kv_s, kv_r, pc_s, pc_r, pz_s, pz_r,
    az_s, az_r, ay_s, ay_r, ac_s, ac_r, ad_s, ad_r, x_s, x_r,
):
    cache = k_ref.shape[0]
    rows = toks * qph
    fresh = 2 * toks
    s_buf = (s0, s1, s2, s3)
    p_buf = (p0, p1, p2, p3)
    me = lax.axis_index("seq")
    my_head = lax.axis_index("head")
    c = lax.rem(me, 2)
    y = lax.rem(me // 2, 2)
    z = me // 4
    core_peer = me + 1 - 2 * c
    y_peer = me + 2 - 4 * y

    def seq_id(other):
        return {"seq": other}

    def zdev(other):
        return other * 4 + y * 2 + c

    barrier = pltpu.get_barrier_semaphore()
    pl.semaphore_signal(barrier, inc=1, device_id=seq_id(core_peer), device_id_type=MESH)
    pl.semaphore_signal(barrier, inc=1, device_id=seq_id(y_peer), device_id_type=MESH)
    for d in range(1, zs_count):
        pl.semaphore_signal(
            barrier, inc=1, device_id=seq_id(zdev(lax.rem(z + d, zs_count))), device_id_type=MESH
        )
    for e in range(1, heads):
        pl.semaphore_signal(
            barrier, inc=1, device_id={"head": lax.rem(my_head + e, heads)}, device_id_type=MESH
        )

    q_rows = jnp.concatenate([q_ref[:, h * HD:(h + 1) * HD] for h in range(qph)], axis=0)
    qall[z * 2 + c] = q_rows.astype(F32).T.astype(BF16)
    pl.semaphore_wait(barrier, zs_count + heads)

    def remote(src, dst, send, recv, device):
        return pltpu.make_async_remote_copy(
            src_ref=src, dst_ref=dst, send_sem=send, recv_sem=recv,
            device_id=device, device_id_type=MESH,
        )

    def nearest(j):
        short = jnp.minimum(z, zs_count - 1 - z)
        paired = j <= 2 * short
        away = jnp.where(paired, (j + 1) // 2, j - short)
        up = jnp.where(paired, j % 2 == 0, z == short)
        return z + jnp.where(up, away, -away)

    def q_move(s, step):
        slot = s * 2 + c
        side = (1 - step) // 2
        return remote(
            qall.at[slot], qall.at[slot], qz_s.at[side, s], qz_r.at[s], seq_id(zdev(z + step))
        )

    def q_to_core(s):
        slot = s * 2 + c
        return remote(qall.at[slot], qall.at[slot], qc_s.at[s], qc_r.at[s], seq_id(core_peer))

    can_rise = z < zs_count - 1
    can_fall = z > 0

    @pl.when(can_rise)
    def _():
        q_move(z, 1).start()

    @pl.when(can_fall)
    def _():
        q_move(z, -1).start()

    q_to_core(z).start()

    length = len_ref[0]
    used = lax.broadcasted_iota(jnp.int32, (cache, HD), 0) < length
    k1[...] = jnp.where(used, k_ref[...].astype(F32), k_ref[0:1, :].astype(F32)).astype(BF16)
    nkv[0:toks] = nk_ref[...]
    nkv[toks:fresh] = nv_ref[...]
    k_to_y = remote(k1, k2.at[pl.ds(0, cache)], kv_s.at[0], kv_r.at[0], seq_id(y_peer))
    n_to_y = remote(nkv, nkv_y, kv_s.at[1], kv_r.at[1], seq_id(y_peer))
    v_to_y = remote(v1, v2.at[:, pl.ds(0, cache)], kv_s.at[2], kv_r.at[2], seq_id(y_peer))
    n_to_y.start()
    k_to_y.start()
    v1[0:HD] = jnp.where(used, v_ref[...].astype(F32), 0.0).T.astype(BF16)
    used_lane = lax.broadcasted_iota(jnp.int32, (AUG - HD, cache), 1) < length
    v1[HD:AUG] = jnp.where(used_lane, 1.0, 0.0).astype(BF16)
    v_to_y.start()

    lane = lax.broadcasted_iota(jnp.int32, (1, HD), 1)

    def chip_ranks(chip, half):
        row = rank_ref[pl.ds(chip, 1), :]
        turned = pltpu.roll(row, toks, 1)
        first = jnp.where(lane < toks, row, turned)
        second = jnp.where(lane < toks, turned, row)
        return jnp.where(half == 0, first, second).astype(F32)

    own_chip = z * 2 + y
    both = jnp.where(lane < toks, chip_ranks(own_chip, c), chip_ranks(z * 2 + 1 - y, c))
    krank[...] = jnp.broadcast_to(both, (HD, HD)).T

    half_rows = rows // 2
    parts = (slice(0, half_rows), slice(half_rows, rows))
    stat = lax.broadcasted_iota(jnp.int32, (8, half_rows), 0)

    def staged(count, score, weigh, gather):
        for i in range(count + 2):
            if i < count:
                score(i)
            if 1 <= i <= count:
                weigh(i - 1)
            if i >= 2:
                gather(i - 2)

    def first_pass(slots):
        tiles = [(slot, cols) for slot in slots for cols in parts]
        tops = {}

        def score(i):
            slot, cols = tiles[i]
            s_buf[i][0:cache] = dot(k1[...], qall[slot, :, cols])

        def weigh(i):
            s = s_buf[i][0:cache]
            tops[i] = jnp.max(s, axis=0, keepdims=True)
            p_buf[i][0:cache] = jnp.exp2((s - tops[i]) * SCALE).astype(BF16)

        def gather(i):
            slot, cols = tiles[i]
            summed = dot(v1[...], p_buf[i][0:cache])
            part[slot, 0:HD, cols] = summed[0:HD]
            part[slot, HD:PART, cols] = jnp.where(stat == 0, summed[HD:HD + 1], tops[i])

        staged(len(tiles), score, weigh, gather)

    def second_pass(zz):
        k_rank = jnp.concatenate([krank[...]] * (half_rows // HD), axis=1)
        tiles, usable = [], []
        for half_of in (1 - c, c):
            q_rank = chip_ranks(zz * 2 + y, half_of)
            q_rank = jnp.concatenate([q_rank] * (half_rows // HD), axis=1)
            for cols in parts:
                tiles.append((zz * 2 + half_of, cols))
                usable.append(q_rank)
        old = [
            (part[slot, HD:HD + 1, cols], part[slot, HD + 1:HD + 2, cols]) for slot, cols in tiles
        ]
        tops = {}

        def score(i):
            slot, cols = tiles[i]
            s_buf[i][...] = dot(k2[...], qall[slot, :, cols])

        def weigh(i):
            s = s_buf[i][0:cache]
            s_new = jnp.where(k_rank <= usable[i], s_buf[i][cache:cache + fresh], FILL)
            top = jnp.maximum(jnp.max(s, axis=0, keepdims=True), old[i][1])
            top = jnp.maximum(top, jnp.max(s_new, axis=0, keepdims=True))
            p_buf[i][0:cache] = jnp.exp2((s - top) * SCALE).astype(BF16)
            p_buf[i][cache:cache + fresh] = jnp.exp2((s_new - top) * SCALE).astype(BF16)
            tops[i] = top

        def gather(i):
            slot, cols = tiles[i]
            summed = dot(v2[...], p_buf[i][...])
            keep = jnp.exp2((old[i][1] - tops[i]) * SCALE)
            part[slot, 0:HD, cols] = part[slot, 0:HD, cols] * keep + summed[0:HD]
            total = old[i][0] * keep + summed[HD:HD + 1]
            part[slot, HD:PART, cols] = jnp.where(stat == 0, total, tops[i])

        staged(len(tiles), score, weigh, gather)

    def pass_one(j, carry):
        s = nearest(j)
        step = jnp.where(s < z, 1, -1)

        @pl.when(j > 0)
        def _():
            q_move(s, step).wait_recv()

            @pl.when(jnp.where(s < z, z < zs_count - 1, z > 0))
            def _():
                q_move(s, step).start()

            q_to_core(s).start()

        q_to_core(s).wait_recv()
        first_pass([s * 2 + c, s * 2 + 1 - c])
        return carry

    lax.fori_loop(0, zs_count, pass_one, 0)

    n_to_y.wait_recv()
    k_to_y.wait_recv()
    k2[cache:cache + toks] = nkv[0:toks]
    k2[cache + toks:cache + fresh] = nkv_y[0:toks]
    new_values = jnp.concatenate([nkv[toks:fresh], nkv_y[toks:fresh]], axis=0)
    v_to_y.wait_recv()
    v2[0:HD, cache:cache + fresh] = new_values.astype(F32).T.astype(BF16)
    v2[HD:AUG, cache:cache + fresh] = jnp.ones((AUG - HD, fresh), BF16)

    def p_to_core(d):
        zz = lax.rem(z - d + zs_count, zs_count)
        at = d - 1
        return remote(
            part.at[zz * 2 + 1 - c], corebuf.at[at], pc_s.at[at], pc_r.at[at], seq_id(core_peer)
        )

    def p_to_z(d):
        zz = lax.rem(z - d + zs_count, zs_count)
        return remote(zsend.at[d], zrecv.at[d], pz_s.at[d], pz_r.at[d], seq_id(zdev(zz)))

    def merged(slot, at):
        sum_a, top_a = part[slot, HD:HD + 1, :], part[slot, HD + 1:HD + 2, :]
        sum_b, top_b = corebuf[at, HD:HD + 1, :], corebuf[at, HD + 1:HD + 2, :]
        top = jnp.maximum(top_a, top_b)
        fac_a = jnp.exp2((top_a - top) * SCALE)
        fac_b = jnp.exp2((top_b - top) * SCALE)
        total = sum_a * fac_a + sum_b * fac_b
        level = top * SCALE + jnp.log2(total)
        inverse = 1.0 / total
        mean = part[slot, 0:HD, :] * (fac_a * inverse) + corebuf[at, 0:HD, :] * (fac_b * inverse)
        return mean, level

    def pass_two(d, carry):
        @pl.when(d <= zs_count)
        def _():
            second_pass(lax.rem(z - d + zs_count, zs_count))
            p_to_core(d).start()

        @pl.when(d > 1)
        def _():
            at = d - 1
            zz = lax.rem(z - at + zs_count, zs_count)
            p_to_core(at).wait_recv()

            @pl.when(at < zs_count)
            def _():
                mean, level = merged(zz * 2 + c, at - 1)
                zsend[at, 0:HD] = mean.astype(BF16)
                high = level.astype(BF16).astype(F32)
                middle = (level - high).astype(BF16).astype(F32)
                low = level - high - middle
                place = lax.broadcasted_iota(jnp.int32, (AUG - HD, rows), 0)
                terms = jnp.where(place == 0, high, jnp.where(place == 1, middle, low))
                zsend[at, HD:AUG] = terms.astype(BF16)
                p_to_z(at).start()

        return carry

    lax.fori_loop(1, zs_count + 2, pass_two, 0)

    means, levels = [], []
    mean, level = merged(z * 2 + c, zs_count - 1)
    means.append(mean)
    levels.append(level)
    for d in range(1, zs_count):
        p_to_z(d).wait_recv()
        terms = zrecv[d, HD:AUG].astype(F32)
        levels.append(terms[0:1] + terms[1:2] + terms[2:3])
        means.append(zrecv[d, 0:HD].astype(F32))
    top = functools.reduce(jnp.maximum, levels)
    factors = [jnp.exp2(level - top) for level in levels]
    inverse = 1.0 / sum(factors)
    attended = sum(mean * (factor * inverse) for mean, factor in zip(means, factors))
    attended = attended.T.astype(BF16)
    own = pl.ds(pl.multiple_of(me * toks, toks), toks)
    for h in range(qph):
        aall[own, h * HD:(h + 1) * HD] = attended[h * toks:(h + 1) * toks]

    chip_rows = 4 * toks
    per_head = zs_count // heads

    def spot(zz, yy, cc):
        return pl.ds(pl.multiple_of((zz * 4 + yy * 2 + cc) * toks, toks), toks)

    def a_move(s, step):
        where = spot(s, y, c)
        side = 0 if step > 0 else 1
        return remote(
            aall.at[where], aall.at[where], az_s.at[side, s], az_r.at[s], seq_id(zdev(z + step))
        )

    def a_to_y(s):
        where = spot(s, y, c)
        return remote(aall.at[where], aall.at[where], ay_s.at[s], ay_r.at[s], seq_id(y_peer))

    def a_to_core(s):
        where = spot(s, y, c)
        return remote(aall.at[where], aall.at[where], ac_s.at[s], ac_r.at[s], seq_id(core_peer))

    def ay_to_core(s):
        where = spot(s, 1 - y, c)
        return remote(aall.at[where], aall.at[where], ad_s.at[s], ad_r.at[s], seq_id(core_peer))

    def x_send(s):
        owner = s // per_head
        slot = lax.rem(my_head - owner + heads, heads) * per_head + lax.rem(s, per_head)
        return remote(xs.at[s], xr.at[slot], x_s.at[s], x_r.at[slot], {"head": owner})

    def product(s):
        lines = pl.ds(pl.multiple_of(s * chip_rows, chip_rows), chip_rows)
        return dot(aall[lines, :], w_ref[...])

    @pl.when(z < zs_count - 1)
    def _():
        a_move(z, 1).start()

    @pl.when(z > 0)
    def _():
        a_move(z, -1).start()

    a_to_y(z).start()
    a_to_core(z).start()

    def spread(i, carry):
        for step in (1, -1):
            s = z - step * i
            here = jnp.logical_and(s >= 0, s < zs_count)

            @pl.when(jnp.logical_and(here, i < zs_count))
            def _():
                a_move(s, step).wait_recv()
                onward = z < zs_count - 1 if step > 0 else z > 0

                @pl.when(onward)
                def _():
                    a_move(s, step).start()

                a_to_y(s).start()
                a_to_core(s).start()

        for step in (1, -1):
            s = z - step * (i - 1)
            here = jnp.logical_and(s >= 0, s < zs_count)
            if step < 0:
                here = jnp.logical_and(here, i > 1)

            @pl.when(here)
            def _():
                a_to_y(s).wait_recv()
                ay_to_core(s).start()

        for step in (1, -1):
            s = z - step * (i - 2)
            here = jnp.logical_and(jnp.logical_and(s >= 0, s < zs_count), i >= 2)
            if step < 0:
                here = jnp.logical_and(here, i > 2)

            @pl.when(jnp.logical_and(here, s // per_head != my_head))
            def _():
                a_to_core(s).wait_recv()
                ay_to_core(s).wait_recv()
                xs[s] = product(s).astype(BF16)
                x_send(s).start()

        return carry

    lax.fori_loop(1, zs_count + 2, spread, 0)

    for k in range(per_head):
        s = my_head * per_head + k
        a_to_core(s).wait_recv()
        ay_to_core(s).wait_recv()
        facc[k] = product(s)

    for k in range(per_head):
        total = facc[k]
        for e in range(1, heads):
            slot = e * per_head + k
            remote(
                xs.at[0], xr.at[slot], x_s.at[0], x_r.at[slot],
                {"head": lax.rem(my_head + e, heads)},
            ).wait_recv()
            total = total + xr[slot].astype(F32)
        out_ref[k * chip_rows:(k + 1) * chip_rows] = total.astype(BF16)

    n_to_y.wait_send()
    k_to_y.wait_send()
    v_to_y.wait_send()

    def finish(d, carry):
        q_to_core(d).wait_send()
        p_to_core(d + 1).wait_send()
        a_to_y(d).wait_send()
        a_to_core(d).wait_send()
        ay_to_core(d).wait_send()

        @pl.when(d > 0)
        def _():
            p_to_z(d).wait_send()

        @pl.when(jnp.logical_and(z < zs_count - 1, d <= z))
        def _():
            q_move(d, 1).wait_send()
            a_move(d, 1).wait_send()

        @pl.when(jnp.logical_and(z > 0, d >= z))
        def _():
            q_move(d, -1).wait_send()
            a_move(d, -1).wait_send()

        @pl.when(d // per_head != my_head)
        def _():
            x_send(d).wait_send()

        return carry

    lax.fori_loop(0, zs_count, finish, 0)


def body(queries, cache_keys, cache_values, new_keys, new_values, cache_len, span_rank, out_weight):
    toks = queries.shape[0]
    qph = queries.shape[1] // HD
    cache = cache_keys.shape[1]
    rows = toks * qph
    width = out_weight.shape[1]
    shards = lax.axis_size("seq")
    heads = lax.axis_size("head")
    zs = shards // 4
    span = span_rank.shape[0]
    out_rows = span // heads
    vmem = pl.BlockSpec(memory_space=pltpu.VMEM)
    smem = pl.BlockSpec(memory_space=pltpu.SMEM)
    sems = [(2, zs)] + [(zs,)] * 3 + [(3,)] * 2 + [(zs,)] * 4 + [(2, zs)] + [(zs,)] * 9
    per_head = zs // heads
    return pl.pallas_call(
        functools.partial(kernel, zs, heads, toks, qph),
        out_shape=jax.ShapeDtypeStruct((out_rows, width), BF16),
        in_specs=[vmem] * 5 + [smem] + [vmem] * 2,
        out_specs=vmem,
        scratch_shapes=[
            pltpu.VMEM((zs * 2, HD, rows), BF16),
            pltpu.VMEM((cache, HD), BF16),
            pltpu.VMEM((AUG, cache), BF16),
            pltpu.VMEM((2 * toks, HD), BF16),
            pltpu.VMEM((cache + 2 * toks, HD), BF16),
            pltpu.VMEM((AUG, cache + 2 * toks), BF16),
            pltpu.VMEM((2 * toks, HD), BF16),
            pltpu.VMEM((HD, HD), F32),
            pltpu.VMEM((zs * 2, PART, rows), F32),
            pltpu.VMEM((zs, PART, rows), F32),
            pltpu.VMEM((zs, AUG, rows), BF16),
            pltpu.VMEM((zs, AUG, rows), BF16),
            pltpu.VMEM((span, qph * HD), BF16),
            pltpu.VMEM((per_head, 4 * toks, width), F32),
            pltpu.VMEM((zs, 4 * toks, width), BF16),
            pltpu.VMEM((zs, 4 * toks, width), BF16),
        ]
        + [pltpu.VMEM((cache + 2 * toks, rows // 2), F32)] * 4
        + [pltpu.VMEM((cache + 2 * toks, rows // 2), BF16)] * 4
        + [pltpu.SemaphoreType.DMA(count) for count in sems],
        compiler_params=pltpu.CompilerParams(
            collective_id=0, has_side_effects=True, vmem_limit_bytes=56 * 1024 * 1024
        ),
    )(
        queries, cache_keys[0], cache_values[0], new_keys, new_values, cache_len,
        span_rank.reshape(span // HD, HD), out_weight,
    )


def solution(mesh):
    return jax.shard_map(
        body,
        mesh=mesh,
        in_specs=(
            P("seq", "head"),
            P("head", "seq", None),
            P("head", "seq", None),
            P("seq", "head"),
            P("seq", "head"),
            P("seq"),
            P(),
            P("head", "seq"),
        ),
        out_specs=P("head", "seq"),
        check_vma=False,
    )
```

```python
import functools
import math

import jax
import jax.numpy as jnp
from jax import lax
from jax.experimental import pallas as pl
from jax.experimental.pallas import tpu as pltpu
from jax.sharding import PartitionSpec as P

MESH = pl.DeviceIdType.MESH
HD = 128
AUG = 144
PART = 136
FILL = -1e30
SCALE = math.log2(math.e) / math.sqrt(HD)
F32 = jnp.float32
BF16 = jnp.bfloat16


def dot(a, b):
    return jnp.dot(a, b, preferred_element_type=F32)


def kernel(
    zs_count, heads, toks, qph,
    q_ref, k_ref, v_ref, nk_ref, nv_ref, len_ref, rank_ref, w_ref, out_ref,
    qall, k1, v1, nkv, k2, v2, nkv_y, krank, part, corebuf, zsend, zrecv, aall, facc, xs, xr,
    s0, s1, s2, s3, p0, p1, p2, p3,
    qz_s, qz_r, qc_s, qc_r, kv_s, kv_r, pc_s, pc_r, pz_s, pz_r,
    az_s, az_r, ay_s, ay_r, ac_s, ac_r, ad_s, ad_r, x_s, x_r,
):
    cache = k_ref.shape[0]
    rows = toks * qph
    fresh = 2 * toks
    s_buf = (s0, s1, s2, s3)
    p_buf = (p0, p1, p2, p3)
    me = lax.axis_index("seq")
    my_head = lax.axis_index("head")
    c = lax.rem(me, 2)
    y = lax.rem(me // 2, 2)
    z = me // 4
    core_peer = me + 1 - 2 * c
    y_peer = me + 2 - 4 * y

    def seq_id(other):
        return {"seq": other}

    def zdev(other):
        return other * 4 + y * 2 + c

    barrier = pltpu.get_barrier_semaphore()
    pl.semaphore_signal(barrier, inc=1, device_id=seq_id(core_peer), device_id_type=MESH)
    pl.semaphore_signal(barrier, inc=1, device_id=seq_id(y_peer), device_id_type=MESH)
    for d in range(1, zs_count):
        pl.semaphore_signal(
            barrier, inc=1, device_id=seq_id(zdev(lax.rem(z + d, zs_count))), device_id_type=MESH
        )
    for e in range(1, heads):
        pl.semaphore_signal(
            barrier, inc=1, device_id={"head": lax.rem(my_head + e, heads)}, device_id_type=MESH
        )

    q_rows = jnp.concatenate([q_ref[:, h * HD:(h + 1) * HD] for h in range(qph)], axis=0)
    qall[z * 2 + c] = q_rows.astype(F32).T.astype(BF16)
    pl.semaphore_wait(barrier, zs_count + heads)

    def remote(src, dst, send, recv, device):
        return pltpu.make_async_remote_copy(
            src_ref=src, dst_ref=dst, send_sem=send, recv_sem=recv,
            device_id=device, device_id_type=MESH,
        )

    def nearest(j):
        short = jnp.minimum(z, zs_count - 1 - z)
        paired = j <= 2 * short
        away = jnp.where(paired, (j + 1) // 2, j - short)
        up = jnp.where(paired, j % 2 == 0, z == short)
        return z + jnp.where(up, away, -away)

    def q_move(s, step):
        slot = s * 2 + c
        side = (1 - step) // 2
        return remote(
            qall.at[slot], qall.at[slot], qz_s.at[side, s], qz_r.at[s], seq_id(zdev(z + step))
        )

    def q_to_core(s):
        slot = s * 2 + c
        return remote(qall.at[slot], qall.at[slot], qc_s.at[s], qc_r.at[s], seq_id(core_peer))

    can_rise = z < zs_count - 1
    can_fall = z > 0

    @pl.when(can_rise)
    def _():
        q_move(z, 1).start()

    @pl.when(can_fall)
    def _():
        q_move(z, -1).start()

    q_to_core(z).start()

    length = len_ref[0]
    used = lax.broadcasted_iota(jnp.int32, (cache, HD), 0) < length
    k1[...] = jnp.where(used, k_ref[...].astype(F32), k_ref[0:1, :].astype(F32)).astype(BF16)
    nkv[0:toks] = nk_ref[...]
    nkv[toks:fresh] = nv_ref[...]
    k_to_y = remote(k1, k2.at[pl.ds(0, cache)], kv_s.at[0], kv_r.at[0], seq_id(y_peer))
    n_to_y = remote(nkv, nkv_y, kv_s.at[1], kv_r.at[1], seq_id(y_peer))
    v_to_y = remote(v1, v2.at[:, pl.ds(0, cache)], kv_s.at[2], kv_r.at[2], seq_id(y_peer))
    n_to_y.start()
    k_to_y.start()
    v1[0:HD] = jnp.where(used, v_ref[...].astype(F32), 0.0).T.astype(BF16)
    used_lane = lax.broadcasted_iota(jnp.int32, (AUG - HD, cache), 1) < length
    v1[HD:AUG] = jnp.where(used_lane, 1.0, 0.0).astype(BF16)
    v_to_y.start()

    lane = lax.broadcasted_iota(jnp.int32, (1, HD), 1)

    def chip_ranks(chip, half):
        row = rank_ref[pl.ds(chip, 1), :]
        turned = pltpu.roll(row, toks, 1)
        first = jnp.where(lane < toks, row, turned)
        second = jnp.where(lane < toks, turned, row)
        return jnp.where(half == 0, first, second).astype(F32)

    own_chip = z * 2 + y
    both = jnp.where(lane < toks, chip_ranks(own_chip, c), chip_ranks(z * 2 + 1 - y, c))
    krank[...] = jnp.broadcast_to(both, (HD, HD)).T

    half_rows = rows // 2
    parts = (slice(0, half_rows), slice(half_rows, rows))
    stat = lax.broadcasted_iota(jnp.int32, (8, half_rows), 0)

    def staged(count, score, weigh, gather):
        for i in range(count + 2):
            if i < count:
                score(i)
            if 1 <= i <= count:
                weigh(i - 1)
            if i >= 2:
                gather(i - 2)

    def first_pass(slots):
        tiles = [(slot, cols) for slot in slots for cols in parts]
        tops = {}

        def score(i):
            slot, cols = tiles[i]
            s_buf[i][0:cache] = dot(k1[...], qall[slot, :, cols])

        def weigh(i):
            s = s_buf[i][0:cache]
            tops[i] = jnp.max(s, axis=0, keepdims=True)
            p_buf[i][0:cache] = jnp.exp2((s - tops[i]) * SCALE).astype(BF16)

        def gather(i):
            slot, cols = tiles[i]
            summed = dot(v1[...], p_buf[i][0:cache])
            part[slot, 0:HD, cols] = summed[0:HD]
            part[slot, HD:PART, cols] = jnp.where(stat == 0, summed[HD:HD + 1], tops[i])

        staged(len(tiles), score, weigh, gather)

    def second_pass(zz, half_of):
        k_rank = jnp.concatenate([krank[...]] * (half_rows // HD), axis=1)
        q_rank = chip_ranks(zz * 2 + y, half_of)
        usable = k_rank <= jnp.concatenate([q_rank] * (half_rows // HD), axis=1)
        tiles = [(zz * 2 + half_of, cols) for cols in parts]
        old = [
            (part[slot, HD:HD + 1, cols], part[slot, HD + 1:HD + 2, cols]) for slot, cols in tiles
        ]
        tops = {}

        def score(i):
            slot, cols = tiles[i]
            s_buf[i][...] = dot(k2[...], qall[slot, :, cols])

        def weigh(i):
            s = s_buf[i][0:cache]
            s_new = jnp.where(usable, s_buf[i][cache:cache + fresh], FILL)
            top = jnp.maximum(jnp.max(s, axis=0, keepdims=True), old[i][1])
            top = jnp.maximum(top, jnp.max(s_new, axis=0, keepdims=True))
            p_buf[i][0:cache] = jnp.exp2((s - top) * SCALE).astype(BF16)
            p_buf[i][cache:cache + fresh] = jnp.exp2((s_new - top) * SCALE).astype(BF16)
            tops[i] = top

        def gather(i):
            slot, cols = tiles[i]
            summed = dot(v2[...], p_buf[i][...])
            keep = jnp.exp2((old[i][1] - tops[i]) * SCALE)
            part[slot, 0:HD, cols] = part[slot, 0:HD, cols] * keep + summed[0:HD]
            total = old[i][0] * keep + summed[HD:HD + 1]
            part[slot, HD:PART, cols] = jnp.where(stat == 0, total, tops[i])

        staged(len(tiles), score, weigh, gather)

    def pass_one(j, carry):
        s = nearest(j)
        step = jnp.where(s < z, 1, -1)

        @pl.when(j > 0)
        def _():
            q_move(s, step).wait_recv()

            @pl.when(jnp.where(s < z, z < zs_count - 1, z > 0))
            def _():
                q_move(s, step).start()

            q_to_core(s).start()

        q_to_core(s).wait_recv()
        first_pass([s * 2 + c, s * 2 + 1 - c])
        return carry

    lax.fori_loop(0, zs_count, pass_one, 0)

    n_to_y.wait_recv()
    k_to_y.wait_recv()
    k2[cache:cache + toks] = nkv[0:toks]
    k2[cache + toks:cache + fresh] = nkv_y[0:toks]
    new_values = jnp.concatenate([nkv[toks:fresh], nkv_y[toks:fresh]], axis=0)
    v_to_y.wait_recv()
    v2[0:HD, cache:cache + fresh] = new_values.astype(F32).T.astype(BF16)
    v2[HD:AUG, cache:cache + fresh] = jnp.ones((AUG - HD, fresh), BF16)

    def p_to_core(d):
        zz = lax.rem(z - d + zs_count, zs_count)
        at = d - 1
        return remote(
            part.at[zz * 2 + 1 - c], corebuf.at[at], pc_s.at[at], pc_r.at[at], seq_id(core_peer)
        )

    def p_to_z(d):
        zz = lax.rem(z - d + zs_count, zs_count)
        return remote(zsend.at[d], zrecv.at[d], pz_s.at[d], pz_r.at[d], seq_id(zdev(zz)))

    def merged(slot, at):
        sum_a, top_a = part[slot, HD:HD + 1, :], part[slot, HD + 1:HD + 2, :]
        sum_b, top_b = corebuf[at, HD:HD + 1, :], corebuf[at, HD + 1:HD + 2, :]
        top = jnp.maximum(top_a, top_b)
        fac_a = jnp.exp2((top_a - top) * SCALE)
        fac_b = jnp.exp2((top_b - top) * SCALE)
        total = sum_a * fac_a + sum_b * fac_b
        level = top * SCALE + jnp.log2(total)
        inverse = 1.0 / total
        mean = part[slot, 0:HD, :] * (fac_a * inverse) + corebuf[at, 0:HD, :] * (fac_b * inverse)
        return mean, level

    def pass_two(d, carry):
        zz = lax.rem(z - d + zs_count, zs_count)
        second_pass(zz, 1 - c)
        p_to_core(d).start()
        second_pass(zz, c)
        p_to_core(d).wait_recv()

        @pl.when(d < zs_count)
        def _():
            mean, level = merged(zz * 2 + c, d - 1)
            zsend[d, 0:HD] = mean.astype(BF16)
            high = level.astype(BF16).astype(F32)
            middle = (level - high).astype(BF16).astype(F32)
            low = level - high - middle
            place = lax.broadcasted_iota(jnp.int32, (AUG - HD, rows), 0)
            terms = jnp.where(place == 0, high, jnp.where(place == 1, middle, low))
            zsend[d, HD:AUG] = terms.astype(BF16)
            p_to_z(d).start()

        return carry

    lax.fori_loop(1, zs_count + 1, pass_two, 0)

    means, levels = [], []
    mean, level = merged(z * 2 + c, zs_count - 1)
    means.append(mean)
    levels.append(level)
    for d in range(1, zs_count):
        p_to_z(d).wait_recv()
        terms = zrecv[d, HD:AUG].astype(F32)
        levels.append(terms[0:1] + terms[1:2] + terms[2:3])
        means.append(zrecv[d, 0:HD].astype(F32))
    top = functools.reduce(jnp.maximum, levels)
    factors = [jnp.exp2(level - top) for level in levels]
    inverse = 1.0 / sum(factors)
    attended = sum(mean * (factor * inverse) for mean, factor in zip(means, factors))
    attended = attended.T.astype(BF16)
    own = pl.ds(pl.multiple_of(me * toks, toks), toks)
    for h in range(qph):
        aall[own, h * HD:(h + 1) * HD] = attended[h * toks:(h + 1) * toks]

    chip_rows = 4 * toks
    per_head = zs_count // heads

    def spot(zz, yy, cc):
        return pl.ds(pl.multiple_of((zz * 4 + yy * 2 + cc) * toks, toks), toks)

    def a_move(s, step):
        where = spot(s, y, c)
        side = 0 if step > 0 else 1
        return remote(
            aall.at[where], aall.at[where], az_s.at[side, s], az_r.at[s], seq_id(zdev(z + step))
        )

    def a_to_y(s):
        where = spot(s, y, c)
        return remote(aall.at[where], aall.at[where], ay_s.at[s], ay_r.at[s], seq_id(y_peer))

    def a_to_core(s):
        where = spot(s, y, c)
        return remote(aall.at[where], aall.at[where], ac_s.at[s], ac_r.at[s], seq_id(core_peer))

    def ay_to_core(s):
        where = spot(s, 1 - y, c)
        return remote(aall.at[where], aall.at[where], ad_s.at[s], ad_r.at[s], seq_id(core_peer))

    def piece(yy):
        return pl.ds(pl.multiple_of(yy * fresh, fresh), fresh)

    def x_send(s, yy):
        owner = s // per_head
        slot = lax.rem(my_head - owner + heads, heads) * per_head + lax.rem(s, per_head)
        return remote(
            xs.at[s, piece(yy)], xr.at[slot, piece(yy)], x_s.at[yy, s], x_r.at[yy, slot],
            {"head": owner},
        )

    def product(s):
        lines = pl.ds(pl.multiple_of(s * chip_rows, chip_rows), chip_rows)
        return dot(aall[lines, :], w_ref[...])

    def share(s, yy):
        first = (s * 2 + yy) * fresh
        result = dot(aall[pl.ds(pl.multiple_of(first, fresh), fresh), :], w_ref[...])
        xs[s, piece(yy)] = result.astype(BF16)
        x_send(s, yy).start()

    @pl.when(z < zs_count - 1)
    def _():
        a_move(z, 1).start()

    @pl.when(z > 0)
    def _():
        a_move(z, -1).start()

    a_to_y(z).start()
    a_to_core(z).start()

    def spread(i, carry):
        for step in (1, -1):
            s = z - step * i
            here = jnp.logical_and(s >= 0, s < zs_count)

            @pl.when(jnp.logical_and(here, i < zs_count))
            def _():
                a_move(s, step).wait_recv()
                onward = z < zs_count - 1 if step > 0 else z > 0

                @pl.when(onward)
                def _():
                    a_move(s, step).start()

                a_to_y(s).start()
                a_to_core(s).start()

        for step in (1, -1):
            s = z - step * (i - 1)
            here = jnp.logical_and(s >= 0, s < zs_count)
            if step < 0:
                here = jnp.logical_and(here, i > 1)

            @pl.when(jnp.logical_and(here, s // per_head != my_head))
            def _():
                a_to_core(s).wait_recv()
                share(s, y)

            @pl.when(here)
            def _():
                a_to_y(s).wait_recv()
                ay_to_core(s).start()

        for step in (1, -1):
            s = z - step * (i - 2)
            here = jnp.logical_and(jnp.logical_and(s >= 0, s < zs_count), i >= 2)
            if step < 0:
                here = jnp.logical_and(here, i > 2)

            @pl.when(jnp.logical_and(here, s // per_head != my_head))
            def _():
                ay_to_core(s).wait_recv()
                share(s, 1 - y)

        return carry

    lax.fori_loop(1, zs_count + 2, spread, 0)

    for k in range(per_head):
        s = my_head * per_head + k
        a_to_core(s).wait_recv()
        ay_to_core(s).wait_recv()
        facc[k] = product(s)

    for k in range(per_head):
        total = facc[k]
        for e in range(1, heads):
            slot = e * per_head + k
            for yy in range(2):
                remote(
                    xs.at[0, piece(yy)], xr.at[slot, piece(yy)], x_s.at[yy, 0], x_r.at[yy, slot],
                    {"head": lax.rem(my_head + e, heads)},
                ).wait_recv()
            total = total + xr[slot].astype(F32)
        out_ref[k * chip_rows:(k + 1) * chip_rows] = total.astype(BF16)

    n_to_y.wait_send()
    k_to_y.wait_send()
    v_to_y.wait_send()

    def finish(d, carry):
        q_to_core(d).wait_send()
        p_to_core(d + 1).wait_send()
        a_to_y(d).wait_send()
        a_to_core(d).wait_send()
        ay_to_core(d).wait_send()

        @pl.when(d > 0)
        def _():
            p_to_z(d).wait_send()

        @pl.when(jnp.logical_and(z < zs_count - 1, d <= z))
        def _():
            q_move(d, 1).wait_send()
            a_move(d, 1).wait_send()

        @pl.when(jnp.logical_and(z > 0, d >= z))
        def _():
            q_move(d, -1).wait_send()
            a_move(d, -1).wait_send()

        @pl.when(d // per_head != my_head)
        def _():
            x_send(d, 0).wait_send()
            x_send(d, 1).wait_send()

        return carry

    lax.fori_loop(0, zs_count, finish, 0)


def body(queries, cache_keys, cache_values, new_keys, new_values, cache_len, span_rank, out_weight):
    toks = queries.shape[0]
    qph = queries.shape[1] // HD
    cache = cache_keys.shape[1]
    rows = toks * qph
    width = out_weight.shape[1]
    shards = lax.axis_size("seq")
    heads = lax.axis_size("head")
    zs = shards // 4
    span = span_rank.shape[0]
    out_rows = span // heads
    vmem = pl.BlockSpec(memory_space=pltpu.VMEM)
    smem = pl.BlockSpec(memory_space=pltpu.SMEM)
    sems = [(2, zs)] + [(zs,)] * 3 + [(3,)] * 2 + [(zs,)] * 4 + [(2, zs)] + [(zs,)] * 7
    sems += [(2, zs)] * 2
    per_head = zs // heads
    return pl.pallas_call(
        functools.partial(kernel, zs, heads, toks, qph),
        out_shape=jax.ShapeDtypeStruct((out_rows, width), BF16),
        in_specs=[vmem] * 5 + [smem] + [vmem] * 2,
        out_specs=vmem,
        scratch_shapes=[
            pltpu.VMEM((zs * 2, HD, rows), BF16),
            pltpu.VMEM((cache, HD), BF16),
            pltpu.VMEM((AUG, cache), BF16),
            pltpu.VMEM((2 * toks, HD), BF16),
            pltpu.VMEM((cache + 2 * toks, HD), BF16),
            pltpu.VMEM((AUG, cache + 2 * toks), BF16),
            pltpu.VMEM((2 * toks, HD), BF16),
            pltpu.VMEM((HD, HD), F32),
            pltpu.VMEM((zs * 2, PART, rows), F32),
            pltpu.VMEM((zs, PART, rows), F32),
            pltpu.VMEM((zs, AUG, rows), BF16),
            pltpu.VMEM((zs, AUG, rows), BF16),
            pltpu.VMEM((span, qph * HD), BF16),
            pltpu.VMEM((per_head, 4 * toks, width), F32),
            pltpu.VMEM((zs, 4 * toks, width), BF16),
            pltpu.VMEM((zs, 4 * toks, width), BF16),
        ]
        + [pltpu.VMEM((cache + 2 * toks, rows // 2), F32)] * 4
        + [pltpu.VMEM((cache + 2 * toks, rows // 2), BF16)] * 4
        + [pltpu.SemaphoreType.DMA(count) for count in sems],
        compiler_params=pltpu.CompilerParams(
            collective_id=0, has_side_effects=True, vmem_limit_bytes=56 * 1024 * 1024
        ),
    )(
        queries, cache_keys[0], cache_values[0], new_keys, new_values, cache_len,
        span_rank.reshape(span // HD, HD), out_weight,
    )


def solution(mesh):
    return jax.shard_map(
        body,
        mesh=mesh,
        in_specs=(
            P("seq", "head"),
            P("head", "seq", None),
            P("head", "seq", None),
            P("seq", "head"),
            P("seq", "head"),
            P("seq"),
            P(),
            P("head", "seq"),
        ),
        out_specs=P("head", "seq"),
        check_vma=False,
    )
```

```python
import functools
import math

import jax
import jax.numpy as jnp
from jax import lax
from jax.experimental import pallas as pl
from jax.experimental.pallas import tpu as pltpu
from jax.sharding import PartitionSpec as P

MESH = pl.DeviceIdType.MESH
HD = 128
AUG = 144
PART = 136
FILL = -1e30
SCALE = math.log2(math.e) / math.sqrt(HD)
F32 = jnp.float32
BF16 = jnp.bfloat16


def dot(a, b):
    return jnp.dot(a, b, preferred_element_type=F32)


def kernel(
    zs_count, heads, toks, qph,
    q_ref, k_ref, v_ref, nk_ref, nv_ref, len_ref, rank_ref, w_ref, out_ref,
    qall, k1, v1, nkv, k2, v2, nkv_y, krank, part, corebuf, zsend, zrecv, aall, facc, xs, xr,
    s0, s1, s2, s3, p0, p1, p2, p3,
    qz_s, qz_r, qc_s, qc_r, kv_s, kv_r, pc_s, pc_r, pz_s, pz_r,
    az_s, az_r, ay_s, ay_r, ac_s, ac_r, ad_s, ad_r, x_s, x_r,
):
    cache = k_ref.shape[0]
    rows = toks * qph
    fresh = 2 * toks
    s_buf = (s0, s1, s2, s3)
    p_buf = (p0, p1, p2, p3)
    me = lax.axis_index("seq")
    my_head = lax.axis_index("head")
    c = lax.rem(me, 2)
    y = lax.rem(me // 2, 2)
    z = me // 4
    core_peer = me + 1 - 2 * c
    y_peer = me + 2 - 4 * y

    def seq_id(other):
        return {"seq": other}

    def zdev(other):
        return other * 4 + y * 2 + c

    barrier = pltpu.get_barrier_semaphore()
    pl.semaphore_signal(barrier, inc=1, device_id=seq_id(core_peer), device_id_type=MESH)
    pl.semaphore_signal(barrier, inc=1, device_id=seq_id(y_peer), device_id_type=MESH)
    for d in range(1, zs_count):
        pl.semaphore_signal(
            barrier, inc=1, device_id=seq_id(zdev(lax.rem(z + d, zs_count))), device_id_type=MESH
        )
    for e in range(1, heads):
        pl.semaphore_signal(
            barrier, inc=1, device_id={"head": lax.rem(my_head + e, heads)}, device_id_type=MESH
        )

    q_rows = jnp.concatenate([q_ref[:, h * HD:(h + 1) * HD] for h in range(qph)], axis=0)
    qall[z * 2 + c] = q_rows.astype(F32).T.astype(BF16)

    length = len_ref[0]
    used = lax.broadcasted_iota(jnp.int32, (cache, HD), 0) < length
    k1[...] = jnp.where(used, k_ref[...].astype(F32), k_ref[0:1, :].astype(F32)).astype(BF16)
    v1[0:HD] = jnp.where(used, v_ref[...].astype(F32), 0.0).T.astype(BF16)
    place_lane = lax.broadcasted_iota(jnp.int32, (AUG - HD, cache), 1)
    v1[HD:AUG] = jnp.where(place_lane < length, 1.0, 0.0).astype(BF16)
    nkv[0:toks] = nk_ref[...]
    nkv[toks:fresh] = nv_ref[...]
    row = lax.broadcasted_iota(jnp.int32, (AUG - HD, HD), 0)
    digits = jnp.where(row == 0, length // 128, lax.rem(length, 128))
    nkv[fresh:fresh + AUG - HD] = digits.astype(F32).astype(BF16)
    pl.semaphore_wait(barrier, zs_count + heads)

    def remote(src, dst, send, recv, device):
        return pltpu.make_async_remote_copy(
            src_ref=src, dst_ref=dst, send_sem=send, recv_sem=recv,
            device_id=device, device_id_type=MESH,
        )

    k_to_y = remote(k1, k2.at[pl.ds(0, cache)], kv_s.at[0], kv_r.at[0], seq_id(y_peer))
    n_to_y = remote(nkv, nkv_y, kv_s.at[1], kv_r.at[1], seq_id(y_peer))
    v_to_y = remote(
        v1.at[pl.ds(0, HD)], v2.at[pl.ds(0, HD), pl.ds(0, cache)],
        kv_s.at[2], kv_r.at[2], seq_id(y_peer),
    )

    def nearest(j):
        short = jnp.minimum(z, zs_count - 1 - z)
        paired = j <= 2 * short
        away = jnp.where(paired, (j + 1) // 2, j - short)
        up = jnp.where(paired, j % 2 == 0, z == short)
        return z + jnp.where(up, away, -away)

    def q_move(s, step):
        slot = s * 2 + c
        side = (1 - step) // 2
        return remote(
            qall.at[slot], qall.at[slot], qz_s.at[side, s], qz_r.at[s], seq_id(zdev(z + step))
        )

    def q_to_core(s):
        slot = s * 2 + c
        return remote(qall.at[slot], qall.at[slot], qc_s.at[s], qc_r.at[s], seq_id(core_peer))

    can_rise = z < zs_count - 1
    can_fall = z > 0

    @pl.when(can_rise)
    def _():
        q_move(z, 1).start()

    @pl.when(can_fall)
    def _():
        q_move(z, -1).start()

    q_to_core(z).start()
    n_to_y.start()
    k_to_y.start()
    v_to_y.start()

    lane = lax.broadcasted_iota(jnp.int32, (1, HD), 1)

    def chip_ranks(chip, half):
        row = rank_ref[pl.ds(chip, 1), :]
        turned = pltpu.roll(row, toks, 1)
        first = jnp.where(lane < toks, row, turned)
        second = jnp.where(lane < toks, turned, row)
        return jnp.where(half == 0, first, second).astype(F32)

    own_chip = z * 2 + y
    both = jnp.where(lane < toks, chip_ranks(own_chip, c), chip_ranks(z * 2 + 1 - y, c))
    krank[...] = jnp.broadcast_to(both, (HD, HD)).T

    half_rows = rows // 2
    parts = (slice(0, half_rows), slice(half_rows, rows))
    stat = lax.broadcasted_iota(jnp.int32, (8, half_rows), 0)

    def staged(count, score, weigh, gather):
        for i in range(count + 2):
            if i < count:
                score(i)
            if 1 <= i <= count:
                weigh(i - 1)
            if i >= 2:
                gather(i - 2)

    def first_pass(slots):
        tiles = [(slot, cols) for slot in slots for cols in parts]
        tops = {}

        def score(i):
            slot, cols = tiles[i]
            s_buf[i][0:cache] = dot(k1[...], qall[slot, :, cols])

        def weigh(i):
            s = s_buf[i][0:cache]
            tops[i] = jnp.max(s, axis=0, keepdims=True)
            p_buf[i][0:cache] = jnp.exp2((s - tops[i]) * SCALE).astype(BF16)

        def gather(i):
            slot, cols = tiles[i]
            summed = dot(v1[...], p_buf[i][0:cache])
            part[slot, 0:HD, cols] = summed[0:HD]
            part[slot, HD:PART, cols] = jnp.where(stat == 0, summed[HD:HD + 1], tops[i])

        staged(len(tiles), score, weigh, gather)

    def second_pass(zz, half_of):
        k_rank = jnp.concatenate([krank[...]] * (half_rows // HD), axis=1)
        q_rank = chip_ranks(zz * 2 + y, half_of)
        usable = k_rank <= jnp.concatenate([q_rank] * (half_rows // HD), axis=1)
        tiles = [(zz * 2 + half_of, cols) for cols in parts]
        old = [
            (part[slot, HD:HD + 1, cols], part[slot, HD + 1:HD + 2, cols]) for slot, cols in tiles
        ]
        tops = {}

        def score(i):
            slot, cols = tiles[i]
            s_buf[i][...] = dot(k2[...], qall[slot, :, cols])

        def weigh(i):
            s = s_buf[i][0:cache]
            s_new = jnp.where(usable, s_buf[i][cache:cache + fresh], FILL)
            top = jnp.maximum(jnp.max(s, axis=0, keepdims=True), old[i][1])
            top = jnp.maximum(top, jnp.max(s_new, axis=0, keepdims=True))
            p_buf[i][0:cache] = jnp.exp2((s - top) * SCALE).astype(BF16)
            p_buf[i][cache:cache + fresh] = jnp.exp2((s_new - top) * SCALE).astype(BF16)
            tops[i] = top

        def gather(i):
            slot, cols = tiles[i]
            summed = dot(v2[...], p_buf[i][...])
            keep = jnp.exp2((old[i][1] - tops[i]) * SCALE)
            part[slot, 0:HD, cols] = part[slot, 0:HD, cols] * keep + summed[0:HD]
            total = old[i][0] * keep + summed[HD:HD + 1]
            part[slot, HD:PART, cols] = jnp.where(stat == 0, total, tops[i])

        staged(len(tiles), score, weigh, gather)

    def pass_one(j, carry):
        s = nearest(j)
        step = jnp.where(s < z, 1, -1)

        @pl.when(j > 0)
        def _():
            q_move(s, step).wait_recv()

            @pl.when(jnp.where(s < z, z < zs_count - 1, z > 0))
            def _():
                q_move(s, step).start()

            q_to_core(s).start()

        q_to_core(s).wait_recv()
        first_pass([s * 2 + c, s * 2 + 1 - c])
        return carry

    lax.fori_loop(0, zs_count, pass_one, 0)

    n_to_y.wait_recv()
    k_to_y.wait_recv()
    k2[cache:cache + toks] = nkv[0:toks]
    k2[cache + toks:cache + fresh] = nkv_y[0:toks]
    new_values = jnp.concatenate([nkv[toks:fresh], nkv_y[toks:fresh]], axis=0)
    digits = nkv_y[fresh:fresh + AUG - HD].astype(F32)
    length_y = digits[0:1, 0:1] * 128.0 + digits[1:2, 0:1]
    used_y = place_lane.astype(F32) < length_y
    v2[HD:AUG, 0:cache] = jnp.where(used_y, 1.0, 0.0).astype(BF16)
    v_to_y.wait_recv()
    v2[0:HD, cache:cache + fresh] = new_values.astype(F32).T.astype(BF16)
    v2[HD:AUG, cache:cache + fresh] = jnp.ones((AUG - HD, fresh), BF16)

    def p_to_core(d):
        zz = lax.rem(z - d + zs_count, zs_count)
        at = d - 1
        return remote(
            part.at[zz * 2 + 1 - c], corebuf.at[at], pc_s.at[at], pc_r.at[at], seq_id(core_peer)
        )

    def p_to_z(d):
        zz = lax.rem(z - d + zs_count, zs_count)
        return remote(zsend.at[d], zrecv.at[d], pz_s.at[d], pz_r.at[d], seq_id(zdev(zz)))

    def merged(slot, at):
        sum_a, top_a = part[slot, HD:HD + 1, :], part[slot, HD + 1:HD + 2, :]
        sum_b, top_b = corebuf[at, HD:HD + 1, :], corebuf[at, HD + 1:HD + 2, :]
        top = jnp.maximum(top_a, top_b)
        fac_a = jnp.exp2((top_a - top) * SCALE)
        fac_b = jnp.exp2((top_b - top) * SCALE)
        total = sum_a * fac_a + sum_b * fac_b
        level = top * SCALE + jnp.log2(total)
        inverse = 1.0 / total
        mean = part[slot, 0:HD, :] * (fac_a * inverse) + corebuf[at, 0:HD, :] * (fac_b * inverse)
        return mean, level

    def pass_two(d, carry):
        zz = lax.rem(z - d + zs_count, zs_count)
        second_pass(zz, 1 - c)
        p_to_core(d).start()
        second_pass(zz, c)
        p_to_core(d).wait_recv()

        @pl.when(d < zs_count)
        def _():
            mean, level = merged(zz * 2 + c, d - 1)
            zsend[d, 0:HD] = mean.astype(BF16)
            high = level.astype(BF16).astype(F32)
            middle = (level - high).astype(BF16).astype(F32)
            low = level - high - middle
            place = lax.broadcasted_iota(jnp.int32, (AUG - HD, rows), 0)
            terms = jnp.where(place == 0, high, jnp.where(place == 1, middle, low))
            zsend[d, HD:AUG] = terms.astype(BF16)
            p_to_z(d).start()

        return carry

    lax.fori_loop(1, zs_count + 1, pass_two, 0)

    means, levels = [], []
    mean, level = merged(z * 2 + c, zs_count - 1)
    means.append(mean)
    levels.append(level)
    for d in range(1, zs_count):
        p_to_z(d).wait_recv()
        terms = zrecv[d, HD:AUG].astype(F32)
        levels.append(terms[0:1] + terms[1:2] + terms[2:3])
        means.append(zrecv[d, 0:HD].astype(F32))
    top = functools.reduce(jnp.maximum, levels)
    factors = [jnp.exp2(level - top) for level in levels]
    inverse = 1.0 / sum(factors)
    attended = sum(mean * (factor * inverse) for mean, factor in zip(means, factors))
    attended = attended.T.astype(BF16)
    own = pl.ds(pl.multiple_of(me * toks, toks), toks)
    for h in range(qph):
        aall[own, h * HD:(h + 1) * HD] = attended[h * toks:(h + 1) * toks]

    chip_rows = 4 * toks
    per_head = zs_count // heads

    def spot(zz, yy, cc):
        return pl.ds(pl.multiple_of((zz * 4 + yy * 2 + cc) * toks, toks), toks)

    def a_move(s, step):
        where = spot(s, y, c)
        side = 0 if step > 0 else 1
        return remote(
            aall.at[where], aall.at[where], az_s.at[side, s], az_r.at[s], seq_id(zdev(z + step))
        )

    def a_to_y(s):
        where = spot(s, y, c)
        return remote(aall.at[where], aall.at[where], ay_s.at[s], ay_r.at[s], seq_id(y_peer))

    def a_to_core(s):
        where = spot(s, y, c)
        return remote(aall.at[where], aall.at[where], ac_s.at[s], ac_r.at[s], seq_id(core_peer))

    def ay_to_core(s):
        where = spot(s, 1 - y, c)
        return remote(aall.at[where], aall.at[where], ad_s.at[s], ad_r.at[s], seq_id(core_peer))

    def piece(yy):
        return pl.ds(pl.multiple_of(yy * fresh, fresh), fresh)

    def x_send(s, yy):
        owner = s // per_head
        slot = lax.rem(my_head - owner + heads, heads) * per_head + lax.rem(s, per_head)
        return remote(
            xs.at[s, piece(yy)], xr.at[slot, piece(yy)], x_s.at[yy, s], x_r.at[yy, slot],
            {"head": owner},
        )

    def product(s):
        lines = pl.ds(pl.multiple_of(s * chip_rows, chip_rows), chip_rows)
        return dot(aall[lines, :], w_ref[...])

    def share(s, yy):
        first = (s * 2 + yy) * fresh
        result = dot(aall[pl.ds(pl.multiple_of(first, fresh), fresh), :], w_ref[...])
        xs[s, piece(yy)] = result.astype(BF16)
        x_send(s, yy).start()

    @pl.when(z < zs_count - 1)
    def _():
        a_move(z, 1).start()

    @pl.when(z > 0)
    def _():
        a_move(z, -1).start()

    a_to_y(z).start()
    a_to_core(z).start()

    def spread(i, carry):
        for step in (1, -1):
            s = z - step * i
            here = jnp.logical_and(s >= 0, s < zs_count)

            @pl.when(jnp.logical_and(here, i < zs_count))
            def _():
                a_move(s, step).wait_recv()
                onward = z < zs_count - 1 if step > 0 else z > 0

                @pl.when(onward)
                def _():
                    a_move(s, step).start()

                a_to_y(s).start()
                a_to_core(s).start()

        for step in (1, -1):
            s = z - step * (i - 1)
            here = jnp.logical_and(s >= 0, s < zs_count)
            if step < 0:
                here = jnp.logical_and(here, i > 1)

            @pl.when(jnp.logical_and(here, s // per_head != my_head))
            def _():
                a_to_core(s).wait_recv()
                share(s, y)

            @pl.when(here)
            def _():
                a_to_y(s).wait_recv()
                ay_to_core(s).start()

        for step in (1, -1):
            s = z - step * (i - 2)
            here = jnp.logical_and(jnp.logical_and(s >= 0, s < zs_count), i >= 2)
            if step < 0:
                here = jnp.logical_and(here, i > 2)

            @pl.when(jnp.logical_and(here, s // per_head != my_head))
            def _():
                ay_to_core(s).wait_recv()
                share(s, 1 - y)

        return carry

    lax.fori_loop(1, zs_count + 2, spread, 0)

    for k in range(per_head):
        s = my_head * per_head + k
        a_to_core(s).wait_recv()
        ay_to_core(s).wait_recv()
        facc[k] = product(s)

    for k in range(per_head):
        total = facc[k]
        for e in range(1, heads):
            slot = e * per_head + k
            for yy in range(2):
                remote(
                    xs.at[0, piece(yy)], xr.at[slot, piece(yy)], x_s.at[yy, 0], x_r.at[yy, slot],
                    {"head": lax.rem(my_head + e, heads)},
                ).wait_recv()
            total = total + xr[slot].astype(F32)
        out_ref[k * chip_rows:(k + 1) * chip_rows] = total.astype(BF16)

    n_to_y.wait_send()
    k_to_y.wait_send()
    v_to_y.wait_send()

    def finish(d, carry):
        q_to_core(d).wait_send()
        p_to_core(d + 1).wait_send()
        a_to_y(d).wait_send()
        a_to_core(d).wait_send()
        ay_to_core(d).wait_send()

        @pl.when(d > 0)
        def _():
            p_to_z(d).wait_send()

        @pl.when(jnp.logical_and(z < zs_count - 1, d <= z))
        def _():
            q_move(d, 1).wait_send()
            a_move(d, 1).wait_send()

        @pl.when(jnp.logical_and(z > 0, d >= z))
        def _():
            q_move(d, -1).wait_send()
            a_move(d, -1).wait_send()

        @pl.when(d // per_head != my_head)
        def _():
            x_send(d, 0).wait_send()
            x_send(d, 1).wait_send()

        return carry

    lax.fori_loop(0, zs_count, finish, 0)


def body(queries, cache_keys, cache_values, new_keys, new_values, cache_len, span_rank, out_weight):
    toks = queries.shape[0]
    qph = queries.shape[1] // HD
    cache = cache_keys.shape[1]
    rows = toks * qph
    width = out_weight.shape[1]
    shards = lax.axis_size("seq")
    heads = lax.axis_size("head")
    zs = shards // 4
    span = span_rank.shape[0]
    out_rows = span // heads
    vmem = pl.BlockSpec(memory_space=pltpu.VMEM)
    smem = pl.BlockSpec(memory_space=pltpu.SMEM)
    sems = [(2, zs)] + [(zs,)] * 3 + [(3,)] * 2 + [(zs,)] * 4 + [(2, zs)] + [(zs,)] * 7
    sems += [(2, zs)] * 2
    per_head = zs // heads
    return pl.pallas_call(
        functools.partial(kernel, zs, heads, toks, qph),
        out_shape=jax.ShapeDtypeStruct((out_rows, width), BF16),
        in_specs=[vmem] * 5 + [smem] + [vmem] * 2,
        out_specs=vmem,
        scratch_shapes=[
            pltpu.VMEM((zs * 2, HD, rows), BF16),
            pltpu.VMEM((cache, HD), BF16),
            pltpu.VMEM((AUG, cache), BF16),
            pltpu.VMEM((2 * toks + AUG - HD, HD), BF16),
            pltpu.VMEM((cache + 2 * toks, HD), BF16),
            pltpu.VMEM((AUG, cache + 2 * toks), BF16),
            pltpu.VMEM((2 * toks + AUG - HD, HD), BF16),
            pltpu.VMEM((HD, HD), F32),
            pltpu.VMEM((zs * 2, PART, rows), F32),
            pltpu.VMEM((zs, PART, rows), F32),
            pltpu.VMEM((zs, AUG, rows), BF16),
            pltpu.VMEM((zs, AUG, rows), BF16),
            pltpu.VMEM((span, qph * HD), BF16),
            pltpu.VMEM((per_head, 4 * toks, width), F32),
            pltpu.VMEM((zs, 4 * toks, width), BF16),
            pltpu.VMEM((zs, 4 * toks, width), BF16),
        ]
        + [pltpu.VMEM((cache + 2 * toks, rows // 2), F32)] * 4
        + [pltpu.VMEM((cache + 2 * toks, rows // 2), BF16)] * 4
        + [pltpu.SemaphoreType.DMA(count) for count in sems],
        compiler_params=pltpu.CompilerParams(
            collective_id=0, has_side_effects=True, vmem_limit_bytes=56 * 1024 * 1024
        ),
    )(
        queries, cache_keys[0], cache_values[0], new_keys, new_values, cache_len,
        span_rank.reshape(span // HD, HD), out_weight,
    )


def solution(mesh):
    return jax.shard_map(
        body,
        mesh=mesh,
        in_specs=(
            P("seq", "head"),
            P("head", "seq", None),
            P("head", "seq", None),
            P("seq", "head"),
            P("seq", "head"),
            P("seq"),
            P(),
            P("head", "seq"),
        ),
        out_specs=P("head", "seq"),
        check_vma=False,
    )
```
